128 devices in a mesh: seq: 16 (over y, z), sect: 8 (over x, core).
Axes of the slice: x: 4, y: 4, z: 4, core: 2. Of those that a mesh axis runs over, the one named last changes fastest.
Arguments:
- tokens: bfloat16 [16384, 4096], P(('seq', 'sect'))
- image_spans: int32 [4, 4, 2], replicated, may hold values from 0 to 3840, as said below
- proj_weight: bfloat16 [8, 4096, 1536], P('sect')
- out_grad: bfloat16 [16384, 2048], P('seq', 'sect'), may hold values from -6 to 6
Outputs:
- attention: bfloat16 [16384, 2048], P('seq', 'sect')
- grad_weight: float32 [8, 4096, 1536], P('sect', 'seq')
The draws below stay inside these ranges and needn't reach their ends.
Inputs may be any that keep to these rules, and one draw needn't show every extreme that they name: `image_spans`: entry [b, i] = (start, tiles) of image i of sequence b: it covers positions start to start + tiles * 256 - 1 with 1 to 4 tiles, start is a multiple of 128, and it lies within positions i * 1024 to (i + 1) * 1024 - 1; images are disjoint; every other position is text. Some image has 4 tiles.
All inputs are finite; a program needn't handle non-finite values.
Results may differ from the reference program's by a relative error of at most 0.023.
The reference program's roundings to bfloat16 on the way count: a program that leaves them out, or rounds other values in their place, can miss the bound.
Values may be sent and summed in bfloat16 or wider, within the bound.
No kernel may reach another device: no remote copies, remote signals or barrier semaphores. Data moves between devices by JAX's collectives and lax.ppermute only.
A program may use at most 192 MiB of HBM per device.

```python
import jax
import jax.numpy as jnp
from jax import lax

D = 4096
NH = 16
HS = 128
LEN = 4096
IMGS = 4
TILE_TOK = 256
MAXT = 4
ALIGN = 128
TOKENS = 16384
SEQS = 4
BLOCK = 1024
HPO = 2
N_SEQ = 16
N_SECT = 8


def draw_tokens(key, part):
    key = jax.random.fold_in(key, 3)
    key_rows, key_values = jax.random.split(key, 2)
    scales = jnp.exp(jax.random.uniform(key_rows, (TOKENS, 1), minval=0.0, maxval=jnp.log(10.0)))
    values = jax.random.normal(key_values, (TOKENS, D))
    return (values * scales).astype(jnp.bfloat16)


def draw_proj_weight(key, part):
    key = jax.random.fold_in(key, 5)
    key_base = jax.random.fold_in(key, 0)
    full_shape = (N_SECT, D, 2, NH // N_SECT, 3, HS)
    spread = D ** (-0.5)
    base_values = jax.random.normal(key_base, full_shape) * spread
    return base_values.reshape(N_SECT, D, 6 * (NH // N_SECT) * HS).astype(jnp.bfloat16)


def draw_image_spans(key, part):
    key = jax.random.fold_in(key, 7)
    key_tiles, key_offset = jax.random.split(key)
    tiles = jax.random.randint(key_tiles, (SEQS, IMGS), 1, MAXT + 1)
    tiles = tiles.at[0, 0].set(MAXT).at[SEQS - 1, IMGS - 1].set(1)
    slot_length = LEN // IMGS
    room_count = (slot_length - tiles * TILE_TOK) // ALIGN + 1
    offset = jax.random.randint(key_offset, (SEQS, IMGS), 0, 1 << 20) % room_count
    offset = offset.at[SEQS - 1, IMGS - 1].set(room_count[SEQS - 1, IMGS - 1] - 1)
    begins = jnp.arange(IMGS, dtype=jnp.int32)[None, :] * slot_length + offset * ALIGN
    return jnp.stack([begins, tiles], axis=-1).astype(jnp.int32)


def block_scale(key, dims, shards, smallest, high):
    factor_of, own = 1.0, jax.random.fold_in(key, 6)
    for dim, blocks in shards:
        draws = jnp.exp(jax.random.uniform(jax.random.fold_in(own, dim), (blocks,), jnp.float32, smallest / len(shards), high / len(shards)))
        factor_of = factor_of * jnp.repeat(draws, dims[dim] // blocks).reshape([-1 if axis == dim else 1 for axis in range(len(dims))])
    return factor_of


def noise(stream_key, extent, scale, bound, shards=(), held_as=jnp.bfloat16):
    values = jax.random.normal(stream_key, extent, jnp.float32) * scale
    if len(shards) > 0:
        values = block_scale(stream_key, extent, shards, -0.22, 0.18) * values
    return jnp.clip(values, min=-bound, max=bound).astype(held_as)


def setup_inputs(seed: int = 0) -> dict:
    seeds = jax.random.split(jax.random.key(seed), 5)
    tokens = draw_tokens(jax.random.fold_in(seeds[4], 71), 0)
    image_spans = draw_image_spans(jax.random.fold_in(seeds[4], 71), 0)
    proj_weight = draw_proj_weight(jax.random.fold_in(seeds[4], 71), 0)
    out_grad = noise(seeds[3], (TOKENS, NH * HS), 1.0, 6.0, ((0, 16), (1, 8)))
    return dict(tokens=tokens, image_spans=image_spans, proj_weight=proj_weight, out_grad=out_grad)


EPSILON = 1e-05
MASKED = -1e+30

def image_rows(image_spans):
    position = jnp.arange(LEN, dtype=jnp.int32)
    begins = image_spans[:, :, 0]
    beyond = begins + image_spans[:, :, 1] * TILE_TOK
    inside = (position[None, :, None] >= begins[:, None, :]) & (position[None, :, None] < beyond[:, None, :])
    return jnp.any(inside, axis=2).reshape(TOKENS)

def modality_weights(proj_weight):
    groups = N_SECT // 2
    blocks_view = proj_weight.reshape(2, groups, D, 2, HPO, 3, HS)
    blocks_view = jnp.transpose(blocks_view, (0, 2, 3, 1, 4, 5, 6))
    return blocks_view.reshape(2, D, NH * 3 * HS)

def section_layout(gradients):
    groups = N_SECT // 2
    blocks_view = gradients.reshape(2, D, 2, groups, HPO, 3, HS)
    blocks_view = jnp.transpose(blocks_view, (0, 3, 1, 2, 4, 5, 6))
    return blocks_view.reshape(N_SECT, D, 6 * HPO * HS)

def head_pass(operands):
    queries, key_rows, values, grad_out = operands
    factor = HS ** (-0.5)
    causal = jnp.arange(LEN)[:, None] >= jnp.arange(LEN)[None, :]
    scores = jnp.dot(queries, key_rows.T, preferred_element_type=jnp.float32) * factor
    scores = jnp.where(causal, scores, MASKED)
    highest = lax.optimization_barrier(jnp.max(scores, axis=1, keepdims=True))
    denominator = lax.optimization_barrier(jnp.sum(jnp.exp(scores - highest), axis=1, keepdims=True))
    log_total = highest + jnp.log(denominator)
    probability = jnp.where(causal, jnp.exp(scores - log_total), 0.0)
    rounded = probability.astype(jnp.bfloat16)
    attended = jnp.dot(rounded, values, preferred_element_type=jnp.float32).astype(jnp.bfloat16)
    row_dot = lax.optimization_barrier(jnp.sum(grad_out.astype(jnp.float32) * attended.astype(jnp.float32), axis=1, keepdims=True))
    grad_values = jnp.dot(rounded.T, grad_out, preferred_element_type=jnp.float32)
    grad_probs = jnp.dot(grad_out, values.T, preferred_element_type=jnp.float32)
    grad_scores = (probability * (grad_probs - row_dot)).astype(jnp.bfloat16)
    grad_queries = jnp.dot(grad_scores, key_rows, preferred_element_type=jnp.float32) * factor
    grad_keys = jnp.dot(grad_scores.T, queries, preferred_element_type=jnp.float32) * factor
    gradients = jnp.stack([grad_queries, grad_keys, grad_values]).astype(jnp.bfloat16)
    return (attended, gradients)

def reference(tokens, image_spans, proj_weight, out_grad):
    as_float = tokens.astype(jnp.float32)
    normed = (as_float * lax.rsqrt(lax.optimization_barrier(jnp.mean(as_float * as_float, axis=1, keepdims=True)) + EPSILON)).astype(jnp.bfloat16)
    is_image = image_rows(image_spans)
    weights = modality_weights(proj_weight)
    text_part = jnp.dot(normed, weights[0], preferred_element_type=jnp.float32)
    image_part = jnp.dot(normed, weights[1], preferred_element_type=jnp.float32)
    projected = jnp.where(is_image[:, None], image_part, text_part).astype(jnp.bfloat16)
    heads_view = projected.reshape(SEQS, LEN, NH, 3, HS)
    heads_view = jnp.transpose(heads_view, (0, 2, 3, 1, 4)).reshape(SEQS * NH, 3, LEN, HS)
    grad_view = jnp.transpose(out_grad.reshape(SEQS, LEN, NH, HS), (0, 2, 1, 3)).reshape(SEQS * NH, LEN, HS)
    attended, gradients = lax.map(head_pass, (heads_view[:, 0], heads_view[:, 1], heads_view[:, 2], grad_view))
    attention = jnp.transpose(attended.reshape(SEQS, NH, LEN, HS), (0, 2, 1, 3)).reshape(TOKENS, NH * HS)
    grad_qkv = jnp.transpose(gradients.reshape(SEQS, NH, 3, LEN, HS), (0, 3, 1, 2, 4)).reshape(TOKENS, NH * 3 * HS)
    image_mask = is_image[:, None]

    def block_partial(running, block_index):
        first_row = block_index * BLOCK
        block_normed = lax.dynamic_slice_in_dim(normed, first_row, BLOCK, 0)
        grads_rows = lax.dynamic_slice_in_dim(grad_qkv, first_row, BLOCK, 0)
        image_marks = lax.dynamic_slice_in_dim(image_mask, first_row, BLOCK, 0)
        text_grad = jnp.where(image_marks, jnp.zeros_like(grads_rows), grads_rows)
        image_grad = jnp.where(image_marks, grads_rows, jnp.zeros_like(grads_rows))
        text_sum = jnp.dot(block_normed.T, text_grad, preferred_element_type=jnp.float32)
        image_sum = jnp.dot(block_normed.T, image_grad, preferred_element_type=jnp.float32)
        text_sum = lax.optimization_barrier(text_sum.astype(jnp.bfloat16)).astype(jnp.float32)
        image_sum = lax.optimization_barrier(image_sum.astype(jnp.bfloat16)).astype(jnp.float32)
        return (running + jnp.stack([text_sum, image_sum]), None)
    start_sum = jnp.zeros((2, D, NH * 3 * HS), jnp.float32)
    summed, _ = lax.scan(block_partial, start_sum, jnp.arange(N_SEQ, dtype=jnp.int32))
    return (attention, section_layout(summed))
```

```python
import jax
import jax.numpy as jnp
from jax import lax
from jax.experimental import pallas as pl
from jax.experimental.pallas import tpu as pltpu
from jax.sharding import PartitionSpec as P

HS = 128
LEN = 4096
TILE_TOK = 256
ALIGN = 128
EPSILON = 1e-05
MASKED = -1e30
SIDE = 4
CHUNK = 512
LOG2E = 1.4426950408889634


def ring_z(step):
    return [(y * SIDE + z, y * SIDE + (z + step) % SIDE) for y in range(SIDE) for z in range(SIDE)]


def ring_y(step):
    return [(y * SIDE + z, (y + step) % SIDE * SIDE + z) for y in range(SIDE) for z in range(SIDE)]


Z_GROUPS = [[y * SIDE + z for z in range(SIDE)] for y in range(SIDE)]


def from_partner(value):
    count = lax.axis_size("sect")
    return lax.ppermute(value, "sect", [(s, s ^ (count // 2)) for s in range(count)])


def block_is_image(image_spans, first_row, rows):
    position = first_row % LEN + jnp.arange(rows, dtype=jnp.int32)
    spans = lax.dynamic_index_in_dim(image_spans, first_row // LEN, 0, keepdims=False)
    begins = spans[:, 0]
    beyond = begins + spans[:, 1] * TILE_TOK
    inside = (position[:, None] >= begins[None]) & (position[:, None] < beyond[None])
    return jnp.any(inside, axis=1)


def attention_kernel(half_ref, got_ref, grad_ref, back_ref, out_ref, score, out_t, dq_t, dk_sum, dv_sum):
    step = pl.program_id(0)
    rows = LEN // SIDE
    half = half_ref[0]
    chunk = 2 * step + jnp.where(step % 2 == 0, half, 1 - half)
    factor = HS ** (-0.5)

    @pl.when(step == 0)
    def _():
        dk_sum[...] = jnp.zeros_like(dk_sum)
        dv_sum[...] = jnp.zeros_like(dv_sum)

    def unpack(ref, first):
        top = ref[step, pl.ds(first, CHUNK // 2), :HS]
        low = ref[step, pl.ds(first, CHUNK // 2), HS:]
        return jnp.concatenate([top, low], axis=0)

    q = unpack(got_ref, rows)
    grad = unpack(grad_ref, 0)

    def keys(j):
        return got_ref[j // 2, pl.ds(pl.multiple_of(j % 2 * CHUNK, CHUNK), CHUNK), :HS]

    def values(j):
        return got_ref[j // 2, pl.ds(pl.multiple_of(j % 2 * CHUNK, CHUNK), CHUNK), HS:]

    def raw(j):
        return lax.dot_general(keys(j), q, (((1,), (1,)), ((), ())), preferred_element_type=jnp.float32)

    def first_pass(j, top):
        s = raw(j)
        score[j] = s
        return jnp.maximum(top, jnp.max(s, axis=0, keepdims=True))

    diagonal = raw(chunk)
    allowed = lax.broadcasted_iota(jnp.int32, (CHUNK, CHUNK), 0) <= lax.broadcasted_iota(
        jnp.int32, (CHUNK, CHUNK), 1
    )
    diagonal = jnp.where(allowed, diagonal, MASKED)
    score[chunk] = diagonal
    top = lax.fori_loop(0, chunk, first_pass, jnp.max(diagonal, axis=0, keepdims=True))
    out_t[...] = jnp.zeros_like(out_t)

    def second_pass(j, total):
        p = jnp.exp2((score[j] - top) * (factor * LOG2E))
        score[j] = p
        out_t[...] += lax.dot_general(
            values(j), p.astype(jnp.bfloat16), (((0,), (0,)), ((), ())), preferred_element_type=jnp.float32
        )
        return total + jnp.sum(p, axis=0, keepdims=True)

    total = lax.fori_loop(0, chunk + 1, second_pass, jnp.zeros((1, CHUNK), jnp.float32))
    inverse = 1.0 / total
    attended = (out_t[...] * inverse).astype(jnp.bfloat16).astype(jnp.float32)
    grad_t = grad.astype(jnp.float32).T
    row_dot = jnp.sum(attended * grad_t, axis=0, keepdims=True)
    attended = attended.T.astype(jnp.bfloat16)
    out_ref[step, :, :HS] = attended[: CHUNK // 2]
    out_ref[step, :, HS:] = attended[CHUNK // 2 :]
    dq_t[...] = jnp.zeros_like(dq_t)

    def third_pass(j, carry):
        p = score[j] * inverse
        span = pl.ds(pl.multiple_of(j * CHUNK, CHUNK), CHUNK)
        dv_sum[span] += jnp.dot(p.astype(jnp.bfloat16), grad, preferred_element_type=jnp.float32)
        dp = lax.dot_general(values(j), grad, (((1,), (1,)), ((), ())), preferred_element_type=jnp.float32)
        ds = (p * (dp - row_dot)).astype(jnp.bfloat16)
        dk_sum[span] += jnp.dot(ds, q, preferred_element_type=jnp.float32)
        dq_t[...] += lax.dot_general(
            keys(j), ds, (((0,), (0,)), ((), ())), preferred_element_type=jnp.float32
        )
        return carry

    lax.fori_loop(0, chunk + 1, third_pass, 0)
    dq = (dq_t[...] * factor).T.astype(jnp.bfloat16)
    back_ref[step, pl.ds(rows, CHUNK // 2), :HS] = dq[: CHUNK // 2]
    back_ref[step, pl.ds(rows, CHUNK // 2), HS:] = dq[CHUNK // 2 :]

    @pl.when(step == SIDE - 1)
    def _():
        for i in range(SIDE):
            back_ref[i, pl.ds(0, rows), :HS] = (dk_sum[pl.ds(i * rows, rows)] * factor).astype(jnp.bfloat16)
            back_ref[i, pl.ds(0, rows), HS:] = dv_sum[pl.ds(i * rows, rows)].astype(jnp.bfloat16)


def attention_pass(half, got, grad):
    whole = lambda shape: pl.BlockSpec(shape, lambda i, half_ref: (0,) * len(shape))
    return pl.pallas_call(
        attention_kernel,
        grid_spec=pltpu.PrefetchScalarGridSpec(
            num_scalar_prefetch=1,
            grid=(SIDE,),
            in_specs=[whole(got.shape), whole(grad.shape)],
            out_specs=[whole(got.shape), whole(grad.shape)],
            scratch_shapes=[
                pltpu.VMEM((LEN // CHUNK, CHUNK, CHUNK), jnp.float32),
                pltpu.VMEM((HS, CHUNK), jnp.float32),
                pltpu.VMEM((HS, CHUNK), jnp.float32),
                pltpu.VMEM((LEN, HS), jnp.float32),
                pltpu.VMEM((LEN, HS), jnp.float32),
            ],
        ),
        out_shape=[
            jax.ShapeDtypeStruct(got.shape, jnp.bfloat16),
            jax.ShapeDtypeStruct(grad.shape, jnp.bfloat16),
        ],
        compiler_params=pltpu.CompilerParams(vmem_limit_bytes=48 * 1024 * 1024),
        cost_estimate=pl.CostEstimate(flops=14_000_000_000, bytes_accessed=7_000_000, transcendentals=5_000_000),
    )(half, got, grad)


def packed(rows):
    count = rows.shape[0] // 2
    return jnp.concatenate([rows[:count], rows[count:]], axis=1)


def unpacked(tile):
    return jnp.concatenate([tile[:, :HS], tile[:, HS:]], axis=0)


def swap_z(value):
    return lax.all_to_all(value, "seq", 0, 0, axis_index_groups=Z_GROUPS, tiled=False)


def ring_sum(piece, place, forth, back):
    bf = jnp.bfloat16
    far = piece((place + 2) % SIDE).astype(bf)
    cut = far.shape[0] // 2
    from_left = lax.ppermute(far[:cut], "seq", forth)
    from_right = lax.ppermute(far[cut:], "seq", back)
    right = piece((place + 1) % SIDE)
    left = piece((place + 3) % SIDE)
    to_right = jnp.concatenate([right[:cut] + from_left.astype(jnp.float32), right[cut:]], axis=0).astype(bf)
    to_left = jnp.concatenate([left[:cut], left[cut:] + from_right.astype(jnp.float32)], axis=0).astype(bf)
    got_left = lax.ppermute(to_right, "seq", forth)
    got_right = lax.ppermute(to_left, "seq", back)
    return piece(place) + got_left.astype(jnp.float32) + got_right.astype(jnp.float32)


def shards(tokens, image_spans, proj_weight, out_grad):
    section_count = lax.axis_size("sect")
    groups = section_count // 2
    row_index = lax.axis_index("seq")
    place_y, place_z = row_index // SIDE, row_index % SIDE
    modality = lax.axis_index("sect") // groups
    as_float = tokens.astype(jnp.float32)
    normed = (
        as_float * lax.rsqrt(jnp.mean(as_float * as_float, axis=1, keepdims=True) + EPSILON)
    ).astype(jnp.bfloat16)
    gathered = lax.all_gather(normed, "sect", axis=0, tiled=True)
    rows, features = gathered.shape
    weight = proj_weight[0]
    half_width = weight.shape[1] // 2
    slice_rows = features // lax.axis_size("seq")
    sent = lax.dynamic_slice(
        weight, (row_index * slice_rows, (1 - modality) * half_width), (slice_rows, half_width)
    )
    other_weight = lax.all_gather(from_partner(sent), "seq", axis=0, tiled=True)
    own_weight = lax.dynamic_slice_in_dim(weight, modality * half_width, half_width, 1)
    is_own = block_is_image(image_spans, row_index * rows, rows) == (modality == 1)

    odd = place_z % 2
    grads = []
    for j in range(2):
        for a in range(2):
            part = jnp.where(odd == 0, a, 1 - a)
            cut = lax.dynamic_slice(out_grad, (part * CHUNK, j * HS), (CHUNK, HS))
            grads.append(packed(cut))
    grad_got = swap_z(jnp.stack(grads))

    own_part = jnp.dot(gathered, own_weight, preferred_element_type=jnp.float32)
    other_part = jnp.dot(gathered, other_weight, preferred_element_type=jnp.float32)
    projected = jnp.where(is_own[:, None], own_part, other_part).astype(jnp.bfloat16)

    sends = []
    for j in range(2):
        first = j * 3 * HS
        for a in range(2):
            part = jnp.where(odd == 0, a, 1 - a)
            q = lax.dynamic_slice(projected, (part * CHUNK, first), (CHUNK, HS))
            sends.append(jnp.concatenate([projected[:, first + HS : first + 3 * HS], packed(q)], axis=0))
    got = swap_z(jnp.stack(sends))
    back, attended = attention_pass((place_z % 2).astype(jnp.int32).reshape(1), got, grad_got)
    returned = swap_z(back)
    attended = swap_z(attended)

    def ordered(tiles, j):
        even, other = unpacked(tiles[2 * j]), unpacked(tiles[2 * j + 1])
        return jnp.where(odd == 0, jnp.concatenate([even, other], axis=0), jnp.concatenate([other, even], axis=0))

    attention = jnp.concatenate([ordered(attended, j) for j in range(2)], axis=1)
    columns = []
    for j in range(2):
        columns.append(ordered(returned[:, rows:], j))
        pair = returned[2 * j, :rows].astype(jnp.float32) + returned[2 * j + 1, :rows].astype(jnp.float32)
        columns.append(pair.astype(jnp.bfloat16))
    grad_rows = jnp.concatenate(columns, axis=1)
    zero = jnp.zeros_like(grad_rows)
    own_grad = jnp.where(is_own[:, None], grad_rows, zero)
    other_grad = jnp.where(is_own[:, None], zero, grad_rows)
    cube = gathered.reshape(rows, SIDE, SIDE, slice_rows)

    def own_piece(z):
        block = lax.dynamic_index_in_dim(cube, z, 2, keepdims=False)
        return jnp.einsum("ryf,rc->yfc", block, own_grad, preferred_element_type=jnp.float32)

    def other_piece(y):
        block = lax.dynamic_index_in_dim(cube, y, 1, keepdims=False)
        return jnp.einsum("rzf,rc->zfc", block, other_grad, preferred_element_type=jnp.float32)

    own_sum = ring_sum(own_piece, place_z, ring_z(1), ring_z(-1))
    other_sum = ring_sum(other_piece, place_y, ring_y(1), ring_y(-1))

    def last(sums):
        return lambda i: lax.dynamic_index_in_dim(sums, i, 0, keepdims=False)

    own_sum = ring_sum(last(own_sum), place_y, ring_y(1), ring_y(-1))
    other_sum = ring_sum(last(other_sum), place_z, ring_z(1), ring_z(-1))
    partner_sum = from_partner(other_sum.astype(jnp.bfloat16)).astype(jnp.float32)
    lower = jnp.where(modality == 0, own_sum, partner_sum)
    upper = jnp.where(modality == 0, partner_sum, own_sum)
    grad_weight = jnp.concatenate([lower, upper], axis=1)[None]
    return (attention, grad_weight)


def solution(mesh):
    in_specs = (P(("seq", "sect"), None), P(), P("sect", None, None), P("seq", "sect"))
    out_specs = (P("seq", "sect"), P("sect", "seq", None))
    return jax.shard_map(shards, mesh=mesh, in_specs=in_specs, out_specs=out_specs, check_vma=False)
```

```python
import jax
import jax.numpy as jnp
from jax import lax
from jax.experimental import pallas as pl
from jax.experimental.pallas import tpu as pltpu
from jax.sharding import PartitionSpec as P

HS = 128
LEN = 4096
TILE_TOK = 256
ALIGN = 128
EPSILON = 1e-05
MASKED = -1e30
SIDE = 4
ROWS = LEN // SIDE
CHUNK = 512
HEAD = 3 * HS
LOG2E = 1.4426950408889634
BF = jnp.bfloat16
F32 = jnp.float32


def ring_z(step):
    return [(y * SIDE + z, y * SIDE + (z + step) % SIDE) for y in range(SIDE) for z in range(SIDE)]


def ring_y(step):
    return [(y * SIDE + z, (y + step) % SIDE * SIDE + z) for y in range(SIDE) for z in range(SIDE)]


Z_GROUPS = [[y * SIDE + z for z in range(SIDE)] for y in range(SIDE)]
Y_GROUPS = [[y * SIDE + z for y in range(SIDE)] for z in range(SIDE)]


def along(ring):
    return (
        lambda value: lax.ppermute(value, "seq", ring(1)),
        lambda value: lax.ppermute(value, "seq", ring(-1)),
    )


def from_partner(value):
    count = lax.axis_size("sect")
    return lax.ppermute(value, "sect", [(s, s ^ (count // 2)) for s in range(count)])


def tile_flags(image_spans):
    position = ALIGN * jnp.arange(LEN // ALIGN, dtype=jnp.int32)
    begins = image_spans[:, :, 0]
    beyond = begins + image_spans[:, :, 1] * TILE_TOK
    inside = (position[None, :, None] >= begins[:, None]) & (position[None, :, None] < beyond[:, None])
    return jnp.any(inside, axis=2).astype(jnp.int32).reshape(-1, ROWS // ALIGN)


def wrapped(value):
    return lax.rem(value + 2 * SIDE, SIDE)


def constant(shape):
    return pl.BlockSpec(shape, lambda i, *refs: (0,) * len(shape))


def project_kernel(info, flags, x, w, *refs):
    a_near, a_far, b_near, b_far = refs[0:3], refs[3:5], refs[5:8], refs[8:10]
    outs, total, other = refs[10:14], refs[14], refs[15]
    k = pl.program_id(0)
    place_y, place_z = info[0], info[1]
    quarter = ROWS
    small = quarter // SIDE
    shift = wrapped(k - place_y)
    for r, ref in ((0, a_near[0]), (1, a_near[1]), (3, a_near[2])):

        @pl.when(shift == r)
        def _(ref=ref):
            other[:, :HEAD] = ref[...].reshape(quarter, HEAD)

    @pl.when(shift == 2)
    def _():
        other[: quarter // 2, :HEAD] = a_far[0][...].reshape(quarter // 2, HEAD)
        other[quarter // 2 :, :HEAD] = a_far[1][...].reshape(quarter // 2, HEAD)

    for r, ref in ((0, b_near[0]), (1, b_near[1]), (3, b_near[2])):
        place = pl.multiple_of(wrapped(place_z + r) * small, small)
        other[pl.ds(place, small), HEAD:] = ref[k]
    place = pl.multiple_of(wrapped(place_z + 2) * small, small)

    @pl.when(k < SIDE // 2)
    def _():
        other[pl.ds(place, small), HEAD:] = b_far[0][lax.rem(k, 2)]

    @pl.when(k >= SIDE // 2)
    def _():
        other[pl.ds(place, small), HEAD:] = b_far[1][lax.rem(k, 2)]

    @pl.when(k == 0)
    def _():
        total[...] = jnp.zeros_like(total)

    @pl.loop(0, ROWS // (2 * ALIGN))
    def _(pair):
        one, two = flags[2 * pair], flags[2 * pair + 1]
        first = pl.multiple_of(pair * 2 * ALIGN, 2 * ALIGN)

        def add(start, count, weights):
            span = pl.ds(start, count)
            total[span] += jnp.dot(x[span], weights, preferred_element_type=F32)

        @pl.when((one == 1) & (two == 1))
        def _():
            add(first, 2 * ALIGN, w[0])

        @pl.when((one == 0) & (two == 0))
        def _():
            add(first, 2 * ALIGN, other[...])

        @pl.when((one == 1) & (two == 0))
        def _():
            add(first, ALIGN, w[0])
            add(first + ALIGN, ALIGN, other[...])

        @pl.when((one == 0) & (two == 1))
        def _():
            add(first, ALIGN, other[...])
            add(first + ALIGN, ALIGN, w[0])

    @pl.when(k == SIDE - 1)
    def _():
        for d in range(SIDE):
            target = wrapped(place_z + d)
            part = lax.rem(target + place_z, 2)
            for h in range(2):

                @pl.when(target // 2 == h)
                def _(d=d, h=h, part=part):
                    outs[d][:ROWS] = total[:, h * HEAD + HS : (h + 1) * HEAD].astype(BF)
                    for side in range(2):
                        start = pl.multiple_of(part * CHUNK + side * (CHUNK // 2), CHUNK // 2)
                        outs[d][ROWS:, side * HS : (side + 1) * HS] = total[
                            pl.ds(start, CHUNK // 2), h * HEAD : h * HEAD + HS
                        ].astype(BF)


def project(info, flags, gathered, proj_weight, near_a, far_a, near_b, far_b):
    rows, features = gathered.shape
    width = 2 * HEAD
    step = features // SIDE
    packed = (ROWS + CHUNK // 2, 2 * HS)
    pieces = [*near_a, *far_a, *near_b, *far_b]
    return pl.pallas_call(
        project_kernel,
        grid_spec=pltpu.PrefetchScalarGridSpec(
            num_scalar_prefetch=2,
            grid=(SIDE,),
            in_specs=[
                pl.BlockSpec((rows, step), lambda k, info, flags: (0, k)),
                pl.BlockSpec((1, step, width), lambda k, info, flags: (0, k, info[2])),
                *[constant(p.shape) for p in pieces],
            ],
            out_specs=[constant(packed)] * SIDE,
            scratch_shapes=[pltpu.VMEM((rows, width), F32), pltpu.VMEM((step, width), BF)],
        ),
        out_shape=[jax.ShapeDtypeStruct(packed, BF)] * SIDE,
        compiler_params=pltpu.CompilerParams(vmem_limit_bytes=48 * 1024 * 1024),
        cost_estimate=pl.CostEstimate(
            flops=2 * rows * features * width, bytes_accessed=22 << 20, transcendentals=0
        ),
    )(info, flags, gathered, proj_weight, *pieces)


def attention_kernel(info, *refs):
    got, grad_ref = refs[0:SIDE], refs[SIDE]
    backs, out_ref = refs[SIDE + 1 : 2 * SIDE + 1], refs[2 * SIDE + 1]
    key_rows, value_rows, q_rows, score, out_t, dq_t, dk_sum, dv_sum = refs[2 * SIDE + 2 :]
    step = pl.program_id(0)
    place = info[1]
    half = lax.rem(place, 2)
    source = wrapped(place - step)
    chunk = 2 * source + lax.rem(source + half, 2)
    factor = HS ** (-0.5)

    @pl.when(step == 0)
    def _():
        dk_sum[...] = jnp.zeros_like(dk_sum)
        dv_sum[...] = jnp.zeros_like(dv_sum)
        for d in range(SIDE):
            span = pl.ds(pl.multiple_of(wrapped(place - d) * ROWS, ROWS), ROWS)
            key_rows[span] = got[d][:ROWS, :HS]
            value_rows[span] = got[d][:ROWS, HS:]

    for d in range(SIDE):

        @pl.when(step == d)
        def _(d=d):
            q_rows[: CHUNK // 2] = got[d][ROWS:, :HS]
            q_rows[CHUNK // 2 :] = got[d][ROWS:, HS:]

    q = q_rows[...]
    grad = jnp.concatenate([grad_ref[source, :, :HS], grad_ref[source, :, HS:]], axis=0)

    def span_of(j):
        return pl.ds(pl.multiple_of(j * CHUNK, CHUNK), CHUNK)

    def raw(j):
        return lax.dot_general(
            key_rows[span_of(j)], q, (((1,), (1,)), ((), ())), preferred_element_type=F32
        )

    def first_pass(j, top):
        s = raw(j)
        score[j] = s
        return jnp.maximum(top, jnp.max(s, axis=0, keepdims=True))

    diagonal = raw(chunk)
    allowed = lax.broadcasted_iota(jnp.int32, (CHUNK, CHUNK), 0) <= lax.broadcasted_iota(
        jnp.int32, (CHUNK, CHUNK), 1
    )
    diagonal = jnp.where(allowed, diagonal, MASKED)
    score[chunk] = diagonal
    top = lax.fori_loop(0, chunk, first_pass, jnp.max(diagonal, axis=0, keepdims=True))
    out_t[...] = jnp.zeros_like(out_t)

    def second_pass(j, total):
        p = jnp.exp2((score[j] - top) * (factor * LOG2E))
        score[j] = p
        out_t[...] += lax.dot_general(
            value_rows[span_of(j)], p.astype(BF), (((0,), (0,)), ((), ())), preferred_element_type=F32
        )
        return total + jnp.sum(p, axis=0, keepdims=True)

    total = lax.fori_loop(0, chunk + 1, second_pass, jnp.zeros((1, CHUNK), F32))
    inverse = 1.0 / total
    attended = (out_t[...] * inverse).astype(BF).astype(F32)
    grad_t = grad.astype(F32).T
    row_dot = jnp.sum(attended * grad_t, axis=0, keepdims=True)
    attended = attended.T.astype(BF)
    out_ref[source, :, :HS] = attended[: CHUNK // 2]
    out_ref[source, :, HS:] = attended[CHUNK // 2 :]
    dq_t[...] = jnp.zeros_like(dq_t)

    def third_pass(j, carry):
        p = score[j] * inverse
        span = span_of(j)
        dv_sum[span] += jnp.dot(p.astype(BF), grad, preferred_element_type=F32)
        dp = lax.dot_general(
            value_rows[span], grad, (((1,), (1,)), ((), ())), preferred_element_type=F32
        )
        ds = (p * (dp - row_dot)).astype(BF)
        dk_sum[span] += jnp.dot(ds, q, preferred_element_type=F32)
        dq_t[...] += lax.dot_general(
            key_rows[span], ds, (((0,), (0,)), ((), ())), preferred_element_type=F32
        )
        return carry

    lax.fori_loop(0, chunk + 1, third_pass, 0)
    dq = (dq_t[...] * factor).T.astype(BF)
    for d in range(SIDE):

        @pl.when(step == d)
        def _(d=d):
            backs[d][ROWS:, :HS] = dq[: CHUNK // 2]
            backs[d][ROWS:, HS:] = dq[CHUNK // 2 :]

    @pl.when(step == SIDE - 1)
    def _():
        for d in range(SIDE):
            span = pl.ds(pl.multiple_of(wrapped(place - d) * ROWS, ROWS), ROWS)
            backs[d][:ROWS, :HS] = (dk_sum[span] * factor).astype(BF)
            backs[d][:ROWS, HS:] = dv_sum[span].astype(BF)


def attention_pass(info, got, grad):
    shape = got[0].shape
    return pl.pallas_call(
        attention_kernel,
        grid_spec=pltpu.PrefetchScalarGridSpec(
            num_scalar_prefetch=1,
            grid=(SIDE,),
            in_specs=[constant(shape)] * SIDE + [constant(grad.shape)],
            out_specs=[constant(shape)] * SIDE + [constant(grad.shape)],
            scratch_shapes=[
                pltpu.VMEM((LEN, HS), BF),
                pltpu.VMEM((LEN, HS), BF),
                pltpu.VMEM((CHUNK, HS), BF),
                pltpu.VMEM((LEN // CHUNK, CHUNK, CHUNK), F32),
                pltpu.VMEM((HS, CHUNK), F32),
                pltpu.VMEM((HS, CHUNK), F32),
                pltpu.VMEM((LEN, HS), F32),
                pltpu.VMEM((LEN, HS), F32),
            ],
        ),
        out_shape=[jax.ShapeDtypeStruct(shape, BF)] * SIDE + [jax.ShapeDtypeStruct(grad.shape, BF)],
        compiler_params=pltpu.CompilerParams(vmem_limit_bytes=48 * 1024 * 1024),
        cost_estimate=pl.CostEstimate(
            flops=28_000_000_000, bytes_accessed=7_000_000, transcendentals=5_000_000
        ),
    )(info, *got, grad)


def assemble_kernel(info, *refs):
    back, outs = refs[:SIDE], refs[SIDE:]
    for z in range(SIDE):

        @pl.when(info[1] == z)
        def _(z=z):
            ordered = [back[(i - z) % SIDE] for i in range(SIDE)]
            for h in range(2):
                pair = ordered[2 * h : 2 * h + 2]
                outs[h][:, HS:] = (pair[0][:ROWS].astype(F32) + pair[1][:ROWS].astype(F32)).astype(BF)
                for part in range(2):
                    tile = pair[(part + z) % 2]
                    for side in range(2):
                        start = part * CHUNK + side * (CHUNK // 2)
                        outs[h][start : start + CHUNK // 2, :HS] = tile[ROWS:, side * HS : (side + 1) * HS]


def assemble(info, back):
    shape = (ROWS, HEAD)
    return pl.pallas_call(
        assemble_kernel,
        grid_spec=pltpu.PrefetchScalarGridSpec(
            num_scalar_prefetch=1,
            grid=(1,),
            in_specs=[constant(b.shape) for b in back],
            out_specs=[constant(shape)] * 2,
        ),
        out_shape=[jax.ShapeDtypeStruct(shape, BF)] * 2,
        compiler_params=pltpu.CompilerParams(vmem_limit_bytes=32 * 1024 * 1024),
        cost_estimate=pl.CostEstimate(flops=1_000_000, bytes_accessed=4 << 20, transcendentals=0),
    )(info, *back)


def weight_kernel(count, halves, more, place, flags, *refs):
    xs, refs = refs[:count], refs[count:]
    grads, refs = refs[: count * halves], refs[count * halves :]
    before, refs = (refs[0], refs[1:]) if more else (None, refs)
    out, masked = refs
    tiles = ROWS // ALIGN

    @pl.when(pl.program_id(0) == 0)
    def _():
        zero = jnp.zeros((ALIGN, HEAD), BF)
        for n in range(count):
            for t in range(tiles):
                flag = flags[n * tiles + t]
                per = tiles // halves
                rows = grads[n * halves + t // per][(t % per) * ALIGN : (t % per + 1) * ALIGN]
                span = slice(n * ROWS + t * ALIGN, n * ROWS + (t + 1) * ALIGN)
                masked[span, :HEAD] = jnp.where(flag == 1, rows, zero)
                masked[span, HEAD:] = jnp.where(flag == 1, zero, rows)

    total = None
    for n in range(count):
        left = jnp.concatenate([xs[n][s, 0] for s in range(tiles)], axis=1)
        term = jnp.dot(left, masked[n * ROWS : (n + 1) * ROWS], preferred_element_type=F32)
        total = term if total is None else total + term
    if more:
        total = total + before[0]
    out[0] = total


def weight_part(place, members, flags, turned, grads, before=None):
    count, halves = len(members), len(grads) // len(members)
    sections, _, features, tile = turned.shape
    piece = features // SIDE
    width = 2 * HEAD

    def block(n):
        return pl.BlockSpec(
            (sections, 1, piece, tile),
            lambda i, place, flags: (0, place[1 + n], wrapped(place[0] + i), 0),
        )

    more = [] if before is None else [before]
    block_out = pl.BlockSpec((1, piece, width), lambda i, place, flags: (i, 0, 0))
    body = lambda *refs: weight_kernel(count, halves, bool(more), *refs)
    scalars = jnp.stack([place, *members]).astype(jnp.int32)
    return pl.pallas_call(
        body,
        grid_spec=pltpu.PrefetchScalarGridSpec(
            num_scalar_prefetch=2,
            grid=(SIDE,),
            in_specs=[*[block(n) for n in range(count)], *[constant(g.shape) for g in grads], *[block_out] * len(more)],
            out_specs=block_out,
            scratch_shapes=[pltpu.VMEM((count * ROWS, width), BF)],
        ),
        out_shape=jax.ShapeDtypeStruct((SIDE, piece, width), F32),
        compiler_params=pltpu.CompilerParams(vmem_limit_bytes=48 * 1024 * 1024),
        cost_estimate=pl.CostEstimate(
            flops=2 * count * ROWS * features * width, bytes_accessed=count * (2 << 20) + (4 << 20), transcendentals=0
        ),
    )(scalars, flags, *[turned] * count, *grads, *more)


def ring_near(value, moves):
    forth, back = moves
    return back(value), forth(value)


def ring_far(nearest, moves):
    following, previous = nearest
    forth, back = moves
    cut = following.shape[0] // 2
    return forth(previous[:cut]), back(following[cut:])


def ring_order(value, nearest, far, place):
    following, previous = nearest
    stack = [value[None], following[None], jnp.concatenate(far, axis=0)[None], previous[None]]
    return lax.dynamic_slice_in_dim(jnp.concatenate(stack * 2, axis=0), wrapped(-place), SIDE, 0)


def ring_sum(pieces, moves):
    forth, back = moves
    far = pieces[2].astype(BF)
    cut = far.shape[0] // 2
    from_left, from_right = forth(far[:cut]), back(far[cut:])
    right, left = pieces[1], pieces[3]
    to_right = jnp.concatenate([right[:cut] + from_left.astype(F32), right[cut:]], axis=0).astype(BF)
    to_left = jnp.concatenate([left[:cut], left[cut:] + from_right.astype(F32)], axis=0).astype(BF)
    got_left, got_right = forth(to_right), back(to_left)
    return pieces[0] + got_left.astype(F32) + got_right.astype(F32)


def packed(rows):
    count = rows.shape[0] // 2
    return jnp.concatenate([rows[:count], rows[count:]], axis=1)


def unpacked(tile):
    return jnp.concatenate([tile[:, :HS], tile[:, HS:]], axis=0)


def exchange(value, groups):
    return lax.all_to_all(value, "seq", 0, 0, axis_index_groups=groups, tiled=False)


def shards(tokens, image_spans, proj_weight, out_grad):
    section_count = lax.axis_size("sect")
    row_index = lax.axis_index("seq")
    place_y, place_z = row_index // SIDE, row_index % SIDE
    modality = lax.axis_index("sect") // (section_count // 2)
    info = jnp.stack([place_y, place_z, modality]).astype(jnp.int32)
    along_y, along_z = along(ring_y), along(ring_z)
    own_flags = (tile_flags(image_spans) == modality).astype(jnp.int32)

    weight = proj_weight[0]
    half_width = weight.shape[1] // 2
    slice_rows = weight.shape[0] // lax.axis_size("seq")
    sent = lax.dynamic_slice(
        weight, (row_index * slice_rows, (1 - modality) * half_width), (slice_rows, half_width)
    )
    got_weight = from_partner(sent)

    as_float = tokens.astype(F32)
    normed = (
        as_float * lax.rsqrt(jnp.mean(as_float * as_float, axis=1, keepdims=True) + EPSILON)
    ).astype(BF)
    gathered = lax.all_gather(normed, "sect", axis=0, tiled=True)
    turned = normed.T
    features, local_rows = turned.shape
    quarter = features // SIDE
    for_z = jnp.transpose(turned.reshape(SIDE, SIDE, slice_rows, local_rows), (1, 0, 2, 3))
    turned_z = exchange(for_z.reshape(SIDE, quarter, local_rows), Z_GROUPS)
    turned_y = exchange(turned.reshape(SIDE, quarter, local_rows), Y_GROUPS)
    turned_z = lax.all_gather(turned_z, "sect", axis=0)
    turned_y = lax.all_gather(turned_y, "sect", axis=0)

    odd = place_z % 2
    grads = []
    for j in range(2):
        for a in range(2):
            part = jnp.where(odd == 0, a, 1 - a)
            grads.append(packed(lax.dynamic_slice(out_grad, (part * CHUNK, j * HS), (CHUNK, HS))))
    grad_got = exchange(jnp.stack(grads), Z_GROUPS)

    one, two = got_weight[:, :HEAD], got_weight[:, HEAD:]
    near_a, near_b = ring_near(one, along_z), ring_near(two, along_y)
    far_a, far_b = ring_far(near_a, along_z), ring_far(near_b, along_y)
    line_a = ring_order(one, near_a, far_a, place_z)
    line_b = ring_order(two, near_b, far_b, place_y)
    near_a, near_b = ring_near(line_a, along_y), ring_near(line_b, along_z)
    far_a, far_b = ring_far(near_a, along_y), ring_far(near_b, along_z)

    flags = lax.dynamic_index_in_dim(own_flags, row_index, 0, keepdims=False)
    sends = project(
        info, flags, gathered, proj_weight, (line_a, *near_a), far_a, (line_b, *near_b), far_b
    )
    got = [sends[0]] + [lax.ppermute(sends[d], "seq", ring_z(d)) for d in range(1, SIDE)]
    *backs, attended = attention_pass(info, got, grad_got)
    returned = [backs[0]] + [lax.ppermute(backs[d], "seq", ring_z(-d)) for d in range(1, SIDE)]
    attended = exchange(attended, Z_GROUPS)

    def ordered(j):
        first, second = unpacked(attended[2 * j]), unpacked(attended[2 * j + 1])
        return jnp.where(
            odd == 0, jnp.concatenate([first, second], axis=0), jnp.concatenate([second, first], axis=0)
        )

    attention = jnp.concatenate([ordered(j) for j in range(2)], axis=1)

    grad_a, grad_b = assemble(info, returned)
    near_a, near_b = ring_near(grad_a, along_z), ring_near(grad_b, along_y)
    far_a, far_b = ring_far(near_a, along_z), ring_far(near_b, along_y)
    flag_cube = own_flags.reshape(SIDE, SIDE, -1)

    def both(shifts, grads_a, grads_b, before_a, before_b):
        along_line = [wrapped(place_z + s) for s in shifts]
        flags_a = jnp.concatenate([flag_cube[place_y, m] for m in along_line])
        part_a = weight_part(place_y, along_line, flags_a, turned_z, grads_a, before_a)
        along_line = [wrapped(place_y + s) for s in shifts]
        flags_b = jnp.concatenate([flag_cube[m, place_z] for m in along_line])
        part_b = weight_part(place_z, along_line, flags_b, turned_y, grads_b, before_b)
        return part_a, part_b

    parts = both([0], [grad_a], [grad_b], None, None)
    parts = both([1, 3], near_a, near_b, *parts)
    parts = both([2], far_a, far_b, *parts)
    sum_a, sum_b = ring_sum(parts[0], along_y), ring_sum(parts[1], along_z)
    others = jnp.concatenate([sum_a[:, HEAD:], sum_b[:, HEAD:]], axis=1).astype(BF)
    theirs = from_partner(others).astype(F32)
    own = jnp.concatenate([sum_a[:, :HEAD], sum_b[:, :HEAD]], axis=1)
    lower = jnp.where(modality == 0, own, theirs)
    upper = jnp.where(modality == 0, theirs, own)
    grad_weight = jnp.concatenate([lower, upper], axis=1)[None]
    return (attention, grad_weight)


def solution(mesh):
    in_specs = (P(("seq", "sect"), None), P(), P("sect", None, None), P("seq", "sect"))
    out_specs = (P("seq", "sect"), P("sect", "seq", None))
    return jax.shard_map(shards, mesh=mesh, in_specs=in_specs, out_specs=out_specs, check_vma=False)
```

```python
import jax
import jax.numpy as jnp
from jax import lax
from jax.experimental import pallas as pl
from jax.experimental.pallas import tpu as pltpu
from jax.sharding import PartitionSpec as P

HS = 128
LEN = 4096
TILE_TOK = 256
ALIGN = 128
EPSILON = 1e-05
MASKED = -1e30
SIDE = 4
ROWS = LEN // SIDE
CHUNK = 512
HEAD = 3 * HS
LOG2E = 1.4426950408889634
BF = jnp.bfloat16
F32 = jnp.float32


def ring_z(step):
    return [(y * SIDE + z, y * SIDE + (z + step) % SIDE) for y in range(SIDE) for z in range(SIDE)]


def ring_y(step):
    return [(y * SIDE + z, (y + step) % SIDE * SIDE + z) for y in range(SIDE) for z in range(SIDE)]


def along(ring):
    return (
        lambda value: lax.ppermute(value, "seq", ring(1)),
        lambda value: lax.ppermute(value, "seq", ring(-1)),
    )


def from_partner(value):
    count = lax.axis_size("sect")
    return lax.ppermute(value, "sect", [(s, s ^ (count // 2)) for s in range(count)])


def tile_flags(image_spans):
    position = ALIGN * jnp.arange(LEN // ALIGN, dtype=jnp.int32)
    begins = image_spans[:, :, 0]
    beyond = begins + image_spans[:, :, 1] * TILE_TOK
    inside = (position[None, :, None] >= begins[:, None]) & (position[None, :, None] < beyond[:, None])
    return jnp.any(inside, axis=2).astype(jnp.int32).reshape(-1, ROWS // ALIGN)


def wrapped(value):
    return lax.rem(value + 2 * SIDE, SIDE)


def constant(shape):
    return pl.BlockSpec(shape, lambda i, *refs: (0,) * len(shape))


def project_kernel(info, flags, x, w, *refs):
    a_near, a_far, b_near, b_far = refs[0:3], refs[3:5], refs[5:8], refs[8:10]
    outs, total, other = refs[10:14], refs[14], refs[15]
    k = pl.program_id(0)
    place_y, place_z = info[0], info[1]
    quarter = ROWS
    small = quarter // SIDE
    shift = wrapped(k - place_y)
    for r, ref in ((0, a_near[0]), (1, a_near[1]), (3, a_near[2])):

        @pl.when(shift == r)
        def _(ref=ref):
            other[:, :HEAD] = ref[...].reshape(quarter, HEAD)

    @pl.when(shift == 2)
    def _():
        other[: quarter // 2, :HEAD] = a_far[0][...].reshape(quarter // 2, HEAD)
        other[quarter // 2 :, :HEAD] = a_far[1][...].reshape(quarter // 2, HEAD)

    for r, ref in ((0, b_near[0]), (1, b_near[1]), (3, b_near[2])):
        place = pl.multiple_of(wrapped(place_z + r) * small, small)
        other[pl.ds(place, small), HEAD:] = ref[k]
    place = pl.multiple_of(wrapped(place_z + 2) * small, small)

    @pl.when(k < SIDE // 2)
    def _():
        other[pl.ds(place, small), HEAD:] = b_far[0][lax.rem(k, 2)]

    @pl.when(k >= SIDE // 2)
    def _():
        other[pl.ds(place, small), HEAD:] = b_far[1][lax.rem(k, 2)]

    @pl.when(k == 0)
    def _():
        total[...] = jnp.zeros_like(total)

    own = w.at[pl.ds(pl.multiple_of(k * quarter, quarter), quarter)]

    @pl.loop(0, ROWS // (2 * ALIGN))
    def _(pair):
        one, two = flags[2 * pair], flags[2 * pair + 1]
        first = pl.multiple_of(pair * 2 * ALIGN, 2 * ALIGN)

        def add(start, count, weights):
            span = pl.ds(start, count)
            total[span] += jnp.dot(x[span], weights[...], preferred_element_type=F32)

        @pl.when((one == 1) & (two == 1))
        def _():
            add(first, 2 * ALIGN, own)

        @pl.when((one == 0) & (two == 0))
        def _():
            add(first, 2 * ALIGN, other)

        @pl.when((one == 1) & (two == 0))
        def _():
            add(first, ALIGN, own)
            add(first + ALIGN, ALIGN, other)

        @pl.when((one == 0) & (two == 1))
        def _():
            add(first, ALIGN, other)
            add(first + ALIGN, ALIGN, own)

    @pl.when(k == SIDE - 1)
    def _():
        for d in range(SIDE):
            target = wrapped(place_z + d)
            part = lax.rem(target + place_z, 2)
            for h in range(2):

                @pl.when(target // 2 == h)
                def _(d=d, h=h, part=part):
                    outs[d][:ROWS] = total[:, h * HEAD + HS : (h + 1) * HEAD].astype(BF)
                    for side in range(2):
                        start = pl.multiple_of(part * CHUNK + side * (CHUNK // 2), CHUNK // 2)
                        outs[d][ROWS:, side * HS : (side + 1) * HS] = total[
                            pl.ds(start, CHUNK // 2), h * HEAD : h * HEAD + HS
                        ].astype(BF)


def project(info, flags, gathered, own_weight, near_a, far_a, near_b, far_b):
    rows, features = gathered.shape
    width = 2 * HEAD
    step = features // SIDE
    packed = (ROWS + CHUNK // 2, 2 * HS)
    pieces = [*near_a, *far_a, *near_b, *far_b]
    return pl.pallas_call(
        project_kernel,
        grid_spec=pltpu.PrefetchScalarGridSpec(
            num_scalar_prefetch=2,
            grid=(SIDE,),
            in_specs=[
                pl.BlockSpec((rows, step), lambda k, info, flags: (0, k)),
                constant(own_weight.shape),
                *[constant(p.shape) for p in pieces],
            ],
            out_specs=[constant(packed)] * SIDE,
            scratch_shapes=[pltpu.VMEM((rows, width), F32), pltpu.VMEM((step, width), BF)],
        ),
        out_shape=[jax.ShapeDtypeStruct(packed, BF)] * SIDE,
        compiler_params=pltpu.CompilerParams(vmem_limit_bytes=32 * 1024 * 1024),
        cost_estimate=pl.CostEstimate(
            flops=2 * rows * features * width, bytes_accessed=22 << 20, transcendentals=0
        ),
    )(info, flags, gathered, own_weight, *pieces)


def attention_kernel(info, *refs):
    got, grad_refs, backs, out_refs = (refs[n * SIDE : (n + 1) * SIDE] for n in range(4))
    key_rows, value_rows, q_rows, g_rows, score, out_t, dq_t, dk_sum, dv_sum = refs[4 * SIDE :]
    step = pl.program_id(0)
    place = info[1]
    half = lax.rem(place, 2)
    source = wrapped(place - step)
    chunk = 2 * source + lax.rem(source + half, 2)
    factor = HS ** (-0.5)

    @pl.when(step == 0)
    def _():
        dk_sum[...] = jnp.zeros_like(dk_sum)
        dv_sum[...] = jnp.zeros_like(dv_sum)
        for d in range(SIDE):
            span = pl.ds(pl.multiple_of(wrapped(place - d) * ROWS, ROWS), ROWS)
            key_rows[span] = got[d][:ROWS, :HS]
            value_rows[span] = got[d][:ROWS, HS:]

    for d in range(SIDE):

        @pl.when(step == d)
        def _(d=d):
            q_rows[: CHUNK // 2] = got[d][ROWS:, :HS]
            q_rows[CHUNK // 2 :] = got[d][ROWS:, HS:]
            g_rows[: CHUNK // 2] = grad_refs[d][:, :HS]
            g_rows[CHUNK // 2 :] = grad_refs[d][:, HS:]

    q = q_rows[...]
    grad = g_rows[...]

    def span_of(j):
        return pl.ds(pl.multiple_of(j * CHUNK, CHUNK), CHUNK)

    def raw(j):
        return lax.dot_general(
            key_rows[span_of(j)], q, (((1,), (1,)), ((), ())), preferred_element_type=F32
        )

    def first_pass(j, top):
        s = raw(j)
        score[j] = s
        return jnp.maximum(top, jnp.max(s, axis=0, keepdims=True))

    diagonal = raw(chunk)
    allowed = lax.broadcasted_iota(jnp.int32, (CHUNK, CHUNK), 0) <= lax.broadcasted_iota(
        jnp.int32, (CHUNK, CHUNK), 1
    )
    diagonal = jnp.where(allowed, diagonal, MASKED)
    score[chunk] = diagonal
    top = lax.fori_loop(0, chunk, first_pass, jnp.max(diagonal, axis=0, keepdims=True))
    out_t[...] = jnp.zeros_like(out_t)

    def second_pass(j, total):
        p = jnp.exp2((score[j] - top) * (factor * LOG2E))
        score[j] = p
        out_t[...] += lax.dot_general(
            value_rows[span_of(j)], p.astype(BF), (((0,), (0,)), ((), ())), preferred_element_type=F32
        )
        return total + jnp.sum(p, axis=0, keepdims=True)

    total = lax.fori_loop(0, chunk + 1, second_pass, jnp.zeros((1, CHUNK), F32))
    inverse = 1.0 / total
    attended = (out_t[...] * inverse).astype(BF).astype(F32)
    grad_t = grad.astype(F32).T
    row_dot = jnp.sum(attended * grad_t, axis=0, keepdims=True)
    attended = attended.T.astype(BF)
    dq_t[...] = jnp.zeros_like(dq_t)

    def third_pass(j, carry):
        p = score[j] * inverse
        span = span_of(j)
        dv_sum[span] += jnp.dot(p.astype(BF), grad, preferred_element_type=F32)
        dp = lax.dot_general(
            value_rows[span], grad, (((1,), (1,)), ((), ())), preferred_element_type=F32
        )
        ds = (p * (dp - row_dot)).astype(BF)
        dk_sum[span] += jnp.dot(ds, q, preferred_element_type=F32)
        dq_t[...] += lax.dot_general(
            key_rows[span], ds, (((0,), (0,)), ((), ())), preferred_element_type=F32
        )
        return carry

    lax.fori_loop(0, chunk + 1, third_pass, 0)
    dq = (dq_t[...] * factor).T.astype(BF)
    for d in range(SIDE):

        @pl.when(step == d)
        def _(d=d):
            backs[d][ROWS:, :HS] = dq[: CHUNK // 2]
            backs[d][ROWS:, HS:] = dq[CHUNK // 2 :]
            out_refs[d][:, :HS] = attended[: CHUNK // 2]
            out_refs[d][:, HS:] = attended[CHUNK // 2 :]

    @pl.when(step == SIDE - 1)
    def _():
        for d in range(SIDE):
            span = pl.ds(pl.multiple_of(wrapped(place - d) * ROWS, ROWS), ROWS)
            backs[d][:ROWS, :HS] = (dk_sum[span] * factor).astype(BF)
            backs[d][:ROWS, HS:] = dv_sum[span].astype(BF)


def attention_pass(info, got, grad):
    shape, small = got[0].shape, (CHUNK // 2, 2 * HS)
    return pl.pallas_call(
        attention_kernel,
        grid_spec=pltpu.PrefetchScalarGridSpec(
            num_scalar_prefetch=1,
            grid=(SIDE,),
            in_specs=[constant(shape)] * SIDE + [constant(small)] * SIDE,
            out_specs=[constant(shape)] * SIDE + [constant(small)] * SIDE,
            scratch_shapes=[
                pltpu.VMEM((LEN, HS), BF),
                pltpu.VMEM((LEN, HS), BF),
                pltpu.VMEM((CHUNK, HS), BF),
                pltpu.VMEM((CHUNK, HS), BF),
                pltpu.VMEM((LEN // CHUNK, CHUNK, CHUNK), F32),
                pltpu.VMEM((HS, CHUNK), F32),
                pltpu.VMEM((HS, CHUNK), F32),
                pltpu.VMEM((LEN, HS), F32),
                pltpu.VMEM((LEN, HS), F32),
            ],
        ),
        out_shape=[jax.ShapeDtypeStruct(shape, BF)] * SIDE + [jax.ShapeDtypeStruct(small, BF)] * SIDE,
        compiler_params=pltpu.CompilerParams(vmem_limit_bytes=48 * 1024 * 1024),
        cost_estimate=pl.CostEstimate(
            flops=28_000_000_000, bytes_accessed=7_000_000, transcendentals=5_000_000
        ),
    )(info, *got, *grad)


def assemble_kernel(info, *refs):
    back, outs = refs[:SIDE], refs[SIDE:]
    for z in range(SIDE):

        @pl.when(info[1] == z)
        def _(z=z):
            ordered = [back[(i - z) % SIDE] for i in range(SIDE)]
            for h in range(2):
                pair = ordered[2 * h : 2 * h + 2]
                outs[h][:, HS:] = (pair[0][:ROWS].astype(F32) + pair[1][:ROWS].astype(F32)).astype(BF)
                for part in range(2):
                    tile = pair[(part + z) % 2]
                    for side in range(2):
                        start = part * CHUNK + side * (CHUNK // 2)
                        outs[h][start : start + CHUNK // 2, :HS] = tile[ROWS:, side * HS : (side + 1) * HS]


def assemble(info, back):
    shape = (ROWS, HEAD)
    return pl.pallas_call(
        assemble_kernel,
        grid_spec=pltpu.PrefetchScalarGridSpec(
            num_scalar_prefetch=1,
            grid=(1,),
            in_specs=[constant(b.shape) for b in back],
            out_specs=[constant(shape)] * 2,
        ),
        out_shape=[jax.ShapeDtypeStruct(shape, BF)] * 2,
        compiler_params=pltpu.CompilerParams(vmem_limit_bytes=32 * 1024 * 1024),
        cost_estimate=pl.CostEstimate(flops=1_000_000, bytes_accessed=4 << 20, transcendentals=0),
    )(info, *back)


def weight_kernel(count, halves, more, place, flags, *refs):
    xs, refs = refs[: 2 * count], refs[2 * count :]
    grads, refs = refs[: 2 * count * halves], refs[2 * count * halves :]
    before, refs = (refs[:2], refs[2:]) if more else (None, refs)
    outs, masked = refs[:2], refs[2]
    tiles = ROWS // ALIGN

    @pl.when(pl.program_id(0) == 0)
    def _():
        zero = jnp.zeros((ALIGN, HEAD), BF)
        for n in range(2 * count):
            for t in range(tiles):
                flag = flags[n * tiles + t]
                per = tiles // halves
                rows = grads[n * halves + t // per][(t % per) * ALIGN : (t % per + 1) * ALIGN]
                span = slice(n * ROWS + t * ALIGN, n * ROWS + (t + 1) * ALIGN)
                masked[span, :HEAD] = jnp.where(flag == 1, rows, zero)
                masked[span, HEAD:] = jnp.where(flag == 1, zero, rows)

    for line in range(2):
        total = None
        for n in range(line * count, (line + 1) * count):
            left = jnp.concatenate([xs[n][s, 0] for s in range(tiles)], axis=1)
            term = jnp.dot(left, masked[n * ROWS : (n + 1) * ROWS], preferred_element_type=F32)
            total = term if total is None else total + term
        if more:
            total = total + before[line][0].astype(F32)
        outs[line][0] = total.astype(BF)


def weight_part(info, shifts, flags, turned, grads, before):
    count, halves = len(shifts), len(grads) // (2 * len(shifts))
    sections, _, features, tile = turned[0].shape
    piece = features // SIDE
    width = 2 * HEAD

    def block(line, shift):
        return pl.BlockSpec(
            (sections, 1, piece, tile),
            lambda i, info, flags: (0, wrapped(info[3] * shift), wrapped(info[line] + info[3] * i), 0),
        )

    block_out = pl.BlockSpec((1, piece, width), lambda i, info, flags: (i, 0, 0))
    body = lambda *refs: weight_kernel(count, halves, bool(before), *refs)
    return pl.pallas_call(
        body,
        grid_spec=pltpu.PrefetchScalarGridSpec(
            num_scalar_prefetch=2,
            grid=(SIDE,),
            in_specs=[
                *[block(line, shift) for line in range(2) for shift in shifts],
                *[constant(g.shape) for g in grads],
                *[block_out] * len(before),
            ],
            out_specs=[block_out] * 2,
            scratch_shapes=[pltpu.VMEM((2 * count * ROWS, width), BF)],
        ),
        out_shape=[jax.ShapeDtypeStruct((SIDE, piece, width), BF)] * 2,
        compiler_params=pltpu.CompilerParams(vmem_limit_bytes=56 * 1024 * 1024),
        cost_estimate=pl.CostEstimate(
            flops=4 * count * ROWS * features * width,
            bytes_accessed=count * (4 << 20) + (6 << 20),
            transcendentals=0,
        ),
    )(info, flags, *[turned[0]] * count, *[turned[1]] * count, *grads, *before)


def ring_near(value, moves):
    forth, back = moves
    return back(value), forth(value)


def ring_far(nearest, moves):
    following, previous = nearest
    forth, back = moves
    cut = following.shape[0] // 2
    return forth(previous[:cut]), back(following[cut:])


def ring_order(value, nearest, far, place):
    following, previous = nearest
    stack = [value[None], following[None], jnp.concatenate(far, axis=0)[None], previous[None]]
    return lax.dynamic_slice_in_dim(jnp.concatenate(stack * 2, axis=0), wrapped(-place), SIDE, 0)


def passing(ring_index, across):
    def move(value):
        pairs = []
        sections = lax.axis_size("sect")
        for member in range(SIDE * SIDE):
            for section in range(sections):
                place = [member // SIDE, member % SIDE]
                place[ring_index] = (place[ring_index] + (1 if section % 2 == 0 else -1)) % SIDE
                target = section ^ (sections // 2) if across else section
                pairs.append((member * sections + section, (place[0] * SIDE + place[1]) * sections + target))
        return lax.ppermute(value, ("seq", "sect"), pairs)

    return move


def pass_sums(lines, moves, moves_across):
    theirs = from_partner(jnp.concatenate([line[0][:, HEAD:] for line in lines], axis=1))
    going = [line[SIDE - 1] for line in lines]
    for n in range(SIDE - 2, 0, -1):
        came = [move(value) for move, value in zip(moves, going)]
        going = [(line[n].astype(F32) + value.astype(F32)).astype(BF) for line, value in zip(lines, came)]
    across = [move(value[:, HEAD:]) for move, value in zip(moves_across, going)]
    came = [move(value[:, :HEAD]) for move, value in zip(moves, going)]
    own = [line[0][:, :HEAD].astype(F32) + value.astype(F32) for line, value in zip(lines, came)]
    theirs = theirs.astype(F32) + jnp.concatenate(across, axis=1).astype(F32)
    return jnp.concatenate(own, axis=1), theirs


def unpacked(tile):
    return jnp.concatenate([tile[:, :HS], tile[:, HS:]], axis=0)


def after(values, *others):
    count = len(values)
    return list(lax.optimization_barrier((*values, *others))[:count])


def spread(pieces, ring):
    return [pieces[0]] + [lax.ppermute(pieces[d], "seq", ring(d)) for d in range(1, SIDE)]


def shards(tokens, image_spans, proj_weight, out_grad):
    section_count = lax.axis_size("sect")
    row_index = lax.axis_index("seq")
    place_y, place_z = row_index // SIDE, row_index % SIDE
    modality = lax.axis_index("sect") // (section_count // 2)
    up = 1 - 2 * (lax.axis_index("sect") % 2)
    info = jnp.stack([place_y, place_z, modality, up]).astype(jnp.int32)
    along_y, along_z = along(ring_y), along(ring_z)
    own_flags = (tile_flags(image_spans) == modality).astype(jnp.int32)

    weight = proj_weight[0]
    half_width = weight.shape[1] // 2
    slice_rows = weight.shape[0] // lax.axis_size("seq")
    sent = lax.dynamic_slice(
        weight, (row_index * slice_rows, (1 - modality) * half_width), (slice_rows, half_width)
    )
    got_weight = from_partner(sent)
    own_weight = lax.dynamic_slice_in_dim(weight, modality * half_width, half_width, 1)

    as_float = tokens.astype(F32)
    normed = (
        as_float * lax.rsqrt(jnp.mean(as_float * as_float, axis=1, keepdims=True) + EPSILON)
    ).astype(BF)
    gathered = lax.all_gather(normed, "sect", axis=0, tiled=True)

    turned = normed.T
    features, local_rows = turned.shape
    quarter = features // SIDE
    cube = turned.reshape(SIDE, SIDE, slice_rows, local_rows)

    def quarter_of(axis, place):
        return lax.dynamic_index_in_dim(cube, wrapped(place), axis, keepdims=False).reshape(quarter, local_rows)

    pieces_z = [quarter_of(1, place_z + d) for d in range(SIDE)]
    pieces_y = [quarter_of(0, place_y + d) for d in range(SIDE)]
    grads = []
    for d in range(SIDE):
        target = wrapped(place_z + d)
        first = (target + place_z) % 2 * CHUNK
        halves = [
            lax.dynamic_slice(out_grad, (first + n * (CHUNK // 2), target // 2 * HS), (CHUNK // 2, HS))
            for n in range(2)
        ]
        grads.append(jnp.concatenate(halves, axis=1))
    came_grad = spread(grads, ring_z)

    (got_weight,) = after([got_weight], *pieces_y, *pieces_z)
    one, two = got_weight[:, :HEAD], got_weight[:, HEAD:]
    near_a, near_b = ring_near(one, along_z), ring_near(two, along_y)
    far_a, far_b = ring_far(near_a, along_z), ring_far(near_b, along_y)
    line_a = ring_order(one, near_a, far_a, place_z)
    line_b = ring_order(two, near_b, far_b, place_y)
    near_a, near_b = ring_near(line_a, along_y), ring_near(line_b, along_z)
    near_a = after(near_a, own_weight)
    far_a, far_b = ring_far(near_a, along_y), ring_far(near_b, along_z)
    far_a = after(far_a, *came_grad)

    flags = lax.dynamic_index_in_dim(own_flags, row_index, 0, keepdims=False)
    came_z = spread(after(pieces_z, *far_a, *far_b), ring_z)
    far_y = lax.ppermute(after([pieces_y[2]], *far_a, *far_b)[0], "seq", ring_y(2))
    sends = project(
        info, flags, gathered, own_weight, (line_a, *near_a), far_a, (line_b, *near_b), far_b
    )
    came_z = after(came_z, sends[0])
    turned_z = lax.all_gather(jnp.stack(came_z), "sect", axis=0)
    got = spread(sends, ring_z)
    near_y = after([pieces_y[1], pieces_y[3]], sends[0])
    near_y = [lax.ppermute(p, "seq", ring_y(d)) for p, d in zip(near_y, (1, 3))]
    stack_y = jnp.stack([pieces_y[0], near_y[0], far_y, near_y[1]])
    turned_y = lax.all_gather(stack_y, "sect", axis=0)
    got = after(got, stack_y)

    results = attention_pass(info, got, came_grad)
    returned = spread(results[:SIDE], lambda d: ring_z(-d))
    grad_a, grad_b = assemble(info, returned)
    flag_cube = own_flags.reshape(SIDE, SIDE, -1)

    def add(shifts, grads, before):
        flags = [flag_cube[place_y, wrapped(place_z - up * s)] for s in shifts]
        flags += [flag_cube[wrapped(place_y - up * s), place_z] for s in shifts]
        grads = [*[g[0] for g in grads], *[g[1] for g in grads]]
        return weight_part(info, shifts, jnp.concatenate(flags), (turned_z, turned_y), grads, before)

    move_y, move_z = passing(0, False), passing(1, False)
    here = (grad_a, grad_b)
    next_1 = (move_z(here[0]), move_y(here[1]))
    next_2 = (move_z(next_1[0]), move_y(next_1[1]))
    parts = add([0, 1], [here, next_1], [])
    next_2 = after(next_2, parts[0])
    next_3 = (move_z(next_2[0]), move_y(next_2[1]))
    parts = add([2], [next_2], parts)
    next_3 = after(next_3, parts[0])
    parts = add([3], [next_3], parts)
    own, theirs = pass_sums(parts, (move_y, move_z), (passing(0, True), passing(1, True)))
    lower = jnp.where(modality == 0, own, theirs)
    upper = jnp.where(modality == 0, theirs, own)
    grad_weight = jnp.concatenate([lower, upper], axis=1)[None]

    attended = spread(after(results[SIDE:], *next_2), lambda d: ring_z(-d))
    by_member = lax.dynamic_slice_in_dim(jnp.stack(attended * 2), wrapped(-place_z), SIDE, 0)
    swapped = place_z % 2

    def ordered(j):
        first, second = unpacked(by_member[2 * j]), unpacked(by_member[2 * j + 1])
        return jnp.where(
            swapped == 0,
            jnp.concatenate([first, second], axis=0),
            jnp.concatenate([second, first], axis=0),
        )

    attention = jnp.concatenate([ordered(j) for j in range(2)], axis=1)
    return (attention, grad_weight)


def solution(mesh):
    in_specs = (P(("seq", "sect"), None), P(), P("sect", None, None), P("seq", "sect"))
    out_specs = (P("seq", "sect"), P("sect", "seq", None))
    return jax.shard_map(shards, mesh=mesh, in_specs=in_specs, out_specs=out_specs, check_vma=False)
```

```python
import jax
import jax.numpy as jnp
from jax import lax
from jax.experimental import pallas as pl
from jax.experimental.pallas import tpu as pltpu
from jax.sharding import PartitionSpec as P

HS = 128
LEN = 4096
TILE_TOK = 256
ALIGN = 128
EPSILON = 1e-05
MASKED = -1e30
SIDE = 4
ROWS = LEN // SIDE
CHUNK = 512
HEAD = 3 * HS
LOG2E = 1.4426950408889634
BF = jnp.bfloat16
F32 = jnp.float32


def ring_z(step):
    return [(y * SIDE + z, y * SIDE + (z + step) % SIDE) for y in range(SIDE) for z in range(SIDE)]


def ring_y(step):
    return [(y * SIDE + z, (y + step) % SIDE * SIDE + z) for y in range(SIDE) for z in range(SIDE)]


def along(ring):
    return (
        lambda value: lax.ppermute(value, "seq", ring(1)),
        lambda value: lax.ppermute(value, "seq", ring(-1)),
    )


def from_partner(value):
    count = lax.axis_size("sect")
    return lax.ppermute(value, "sect", [(s, s ^ (count // 2)) for s in range(count)])


def tile_flags(image_spans):
    position = ALIGN * jnp.arange(LEN // ALIGN, dtype=jnp.int32)
    begins = image_spans[:, :, 0]
    beyond = begins + image_spans[:, :, 1] * TILE_TOK
    inside = (position[None, :, None] >= begins[:, None]) & (position[None, :, None] < beyond[:, None])
    return jnp.any(inside, axis=2).astype(jnp.int32).reshape(-1, ROWS // ALIGN)


def wrapped(value):
    return lax.rem(value + 2 * SIDE, SIDE)


def constant(shape):
    return pl.BlockSpec(shape, lambda i, *refs: (0,) * len(shape))


def project_kernel(info, flags, x, w, *refs):
    a_near, a_far, b_near, b_far = refs[0:3], refs[3:5], refs[5:8], refs[8:10]
    outs, total, other = refs[10:14], refs[14], refs[15]
    k = pl.program_id(0)
    place_y, place_z = info[0], info[1]
    quarter = ROWS
    small = quarter // SIDE
    shift = wrapped(k - place_y)
    for r, ref in ((0, a_near[0]), (1, a_near[1]), (3, a_near[2])):

        @pl.when(shift == r)
        def _(ref=ref):
            other[:, :HEAD] = ref[...].reshape(quarter, HEAD)

    @pl.when(shift == 2)
    def _():
        other[: quarter // 2, :HEAD] = a_far[0][...].reshape(quarter // 2, HEAD)
        other[quarter // 2 :, :HEAD] = a_far[1][...].reshape(quarter // 2, HEAD)

    for r, ref in ((0, b_near[0]), (1, b_near[1]), (3, b_near[2])):
        place = pl.multiple_of(wrapped(place_z + r) * small, small)
        other[pl.ds(place, small), HEAD:] = ref[k]
    place = pl.multiple_of(wrapped(place_z + 2) * small, small)

    @pl.when(k < SIDE // 2)
    def _():
        other[pl.ds(place, small), HEAD:] = b_far[0][lax.rem(k, 2)]

    @pl.when(k >= SIDE // 2)
    def _():
        other[pl.ds(place, small), HEAD:] = b_far[1][lax.rem(k, 2)]

    @pl.when(k == 0)
    def _():
        total[...] = jnp.zeros_like(total)

    own = w.at[pl.ds(pl.multiple_of(k * quarter, quarter), quarter)]

    @pl.loop(0, ROWS // (2 * ALIGN))
    def _(pair):
        one, two = flags[2 * pair], flags[2 * pair + 1]
        first = pl.multiple_of(pair * 2 * ALIGN, 2 * ALIGN)

        def add(start, count, weights):
            span = pl.ds(start, count)
            total[span] += jnp.dot(x[span], weights[...], preferred_element_type=F32)

        @pl.when((one == 1) & (two == 1))
        def _():
            add(first, 2 * ALIGN, own)

        @pl.when((one == 0) & (two == 0))
        def _():
            add(first, 2 * ALIGN, other)

        @pl.when((one == 1) & (two == 0))
        def _():
            add(first, ALIGN, own)
            add(first + ALIGN, ALIGN, other)

        @pl.when((one == 0) & (two == 1))
        def _():
            add(first, ALIGN, other)
            add(first + ALIGN, ALIGN, own)

    @pl.when(k == SIDE - 1)
    def _():
        for d in range(SIDE):
            target = wrapped(place_z + d)
            part = lax.rem(target + place_z, 2)
            for h in range(2):

                @pl.when(target // 2 == h)
                def _(d=d, h=h, part=part):
                    outs[d][:ROWS] = total[:, h * HEAD + HS : (h + 1) * HEAD].astype(BF)
                    for side in range(2):
                        start = pl.multiple_of(part * CHUNK + side * (CHUNK // 2), CHUNK // 2)
                        outs[d][ROWS:, side * HS : (side + 1) * HS] = total[
                            pl.ds(start, CHUNK // 2), h * HEAD : h * HEAD + HS
                        ].astype(BF)


def project(info, flags, gathered, own_weight, near_a, far_a, near_b, far_b):
    rows, features = gathered.shape
    width = 2 * HEAD
    step = features // SIDE
    packed = (ROWS + CHUNK // 2, 2 * HS)
    pieces = [*near_a, *far_a, *near_b, *far_b]
    return pl.pallas_call(
        project_kernel,
        grid_spec=pltpu.PrefetchScalarGridSpec(
            num_scalar_prefetch=2,
            grid=(SIDE,),
            in_specs=[
                pl.BlockSpec((rows, step), lambda k, info, flags: (0, k)),
                constant(own_weight.shape),
                *[constant(p.shape) for p in pieces],
            ],
            out_specs=[constant(packed)] * SIDE,
            scratch_shapes=[pltpu.VMEM((rows, width), F32), pltpu.VMEM((step, width), BF)],
        ),
        out_shape=[jax.ShapeDtypeStruct(packed, BF)] * SIDE,
        compiler_params=pltpu.CompilerParams(vmem_limit_bytes=58 * 1024 * 1024),
        cost_estimate=pl.CostEstimate(
            flops=2 * rows * features * width, bytes_accessed=22 << 20, transcendentals=0
        ),
    )(info, flags, gathered, own_weight, *pieces)


def attention_kernel(info, *refs):
    got, grad_refs, backs, out_refs = (refs[n * SIDE : (n + 1) * SIDE] for n in range(4))
    key_rows, value_rows, q_rows, g_rows, score, out_t, dq_t, dk_sum, dv_sum = refs[4 * SIDE :]
    step = pl.program_id(0)
    place = info[1]
    half = lax.rem(place, 2)
    source = wrapped(place - step)
    chunk = 2 * source + lax.rem(source + half, 2)
    factor = HS ** (-0.5)

    @pl.when(step == 0)
    def _():
        dk_sum[...] = jnp.zeros_like(dk_sum)
        dv_sum[...] = jnp.zeros_like(dv_sum)
        for d in range(SIDE):
            span = pl.ds(pl.multiple_of(wrapped(place - d) * ROWS, ROWS), ROWS)
            key_rows[span] = got[d][:ROWS, :HS]
            value_rows[span] = got[d][:ROWS, HS:]

    for d in range(SIDE):

        @pl.when(step == d)
        def _(d=d):
            q_rows[: CHUNK // 2] = got[d][ROWS:, :HS]
            q_rows[CHUNK // 2 :] = got[d][ROWS:, HS:]
            g_rows[: CHUNK // 2] = grad_refs[d][:, :HS]
            g_rows[CHUNK // 2 :] = grad_refs[d][:, HS:]

    q = q_rows[...]
    grad = g_rows[...]

    def span_of(j):
        return pl.ds(pl.multiple_of(j * CHUNK, CHUNK), CHUNK)

    def raw(j):
        return lax.dot_general(
            key_rows[span_of(j)], q, (((1,), (1,)), ((), ())), preferred_element_type=F32
        )

    def first_pass(j, top):
        s = raw(j)
        score[j] = s
        return jnp.maximum(top, jnp.max(s, axis=0, keepdims=True))

    diagonal = raw(chunk)
    allowed = lax.broadcasted_iota(jnp.int32, (CHUNK, CHUNK), 0) <= lax.broadcasted_iota(
        jnp.int32, (CHUNK, CHUNK), 1
    )
    diagonal = jnp.where(allowed, diagonal, MASKED)
    score[chunk] = diagonal
    top = lax.fori_loop(0, chunk, first_pass, jnp.max(diagonal, axis=0, keepdims=True))
    out_t[...] = jnp.zeros_like(out_t)

    def second_pass(j, total):
        p = jnp.exp2((score[j] - top) * (factor * LOG2E))
        score[j] = p
        out_t[...] += lax.dot_general(
            value_rows[span_of(j)], p.astype(BF), (((0,), (0,)), ((), ())), preferred_element_type=F32
        )
        return total + jnp.sum(p, axis=0, keepdims=True)

    total = lax.fori_loop(0, chunk + 1, second_pass, jnp.zeros((1, CHUNK), F32))
    inverse = 1.0 / total
    attended = (out_t[...] * inverse).astype(BF).astype(F32)
    grad_t = grad.astype(F32).T
    row_dot = jnp.sum(attended * grad_t, axis=0, keepdims=True)
    attended = attended.T.astype(BF)
    dq_t[...] = jnp.zeros_like(dq_t)

    def third_pass(j, carry):
        p = score[j] * inverse
        span = span_of(j)
        dv_sum[span] += jnp.dot(p.astype(BF), grad, preferred_element_type=F32)
        dp = lax.dot_general(
            value_rows[span], grad, (((1,), (1,)), ((), ())), preferred_element_type=F32
        )
        ds = (p * (dp - row_dot)).astype(BF)
        dk_sum[span] += jnp.dot(ds, q, preferred_element_type=F32)
        dq_t[...] += lax.dot_general(
            key_rows[span], ds, (((0,), (0,)), ((), ())), preferred_element_type=F32
        )
        return carry

    lax.fori_loop(0, chunk + 1, third_pass, 0)
    dq = (dq_t[...] * factor).T.astype(BF)
    for d in range(SIDE):

        @pl.when(step == d)
        def _(d=d):
            backs[d][ROWS:, :HS] = dq[: CHUNK // 2]
            backs[d][ROWS:, HS:] = dq[CHUNK // 2 :]
            out_refs[d][:, :HS] = attended[: CHUNK // 2]
            out_refs[d][:, HS:] = attended[CHUNK // 2 :]

    @pl.when(step == SIDE - 1)
    def _():
        for d in range(SIDE):
            span = pl.ds(pl.multiple_of(wrapped(place - d) * ROWS, ROWS), ROWS)
            backs[d][:ROWS, :HS] = (dk_sum[span] * factor).astype(BF)
            backs[d][:ROWS, HS:] = dv_sum[span].astype(BF)


def attention_pass(info, got, grad):
    shape, small = got[0].shape, (CHUNK // 2, 2 * HS)
    return pl.pallas_call(
        attention_kernel,
        grid_spec=pltpu.PrefetchScalarGridSpec(
            num_scalar_prefetch=1,
            grid=(SIDE,),
            in_specs=[constant(shape)] * SIDE + [constant(small)] * SIDE,
            out_specs=[constant(shape)] * SIDE + [constant(small)] * SIDE,
            scratch_shapes=[
                pltpu.VMEM((LEN, HS), BF),
                pltpu.VMEM((LEN, HS), BF),
                pltpu.VMEM((CHUNK, HS), BF),
                pltpu.VMEM((CHUNK, HS), BF),
                pltpu.VMEM((LEN // CHUNK, CHUNK, CHUNK), F32),
                pltpu.VMEM((HS, CHUNK), F32),
                pltpu.VMEM((HS, CHUNK), F32),
                pltpu.VMEM((LEN, HS), F32),
                pltpu.VMEM((LEN, HS), F32),
            ],
        ),
        out_shape=[jax.ShapeDtypeStruct(shape, BF)] * SIDE + [jax.ShapeDtypeStruct(small, BF)] * SIDE,
        compiler_params=pltpu.CompilerParams(vmem_limit_bytes=58 * 1024 * 1024),
        cost_estimate=pl.CostEstimate(
            flops=28_000_000_000, bytes_accessed=7_000_000, transcendentals=5_000_000
        ),
    )(info, *got, *grad)


def assemble_kernel(info, *refs):
    back, outs = refs[:SIDE], refs[SIDE:]
    for z in range(SIDE):

        @pl.when(info[1] == z)
        def _(z=z):
            ordered = [back[(i - z) % SIDE] for i in range(SIDE)]
            for h in range(2):
                pair = ordered[2 * h : 2 * h + 2]
                outs[h][:, HS:] = (pair[0][:ROWS].astype(F32) + pair[1][:ROWS].astype(F32)).astype(BF)
                for part in range(2):
                    tile = pair[(part + z) % 2]
                    for side in range(2):
                        start = part * CHUNK + side * (CHUNK // 2)
                        outs[h][start : start + CHUNK // 2, :HS] = tile[ROWS:, side * HS : (side + 1) * HS]


def assemble(info, back):
    shape = (ROWS, HEAD)
    return pl.pallas_call(
        assemble_kernel,
        grid_spec=pltpu.PrefetchScalarGridSpec(
            num_scalar_prefetch=1,
            grid=(1,),
            in_specs=[constant(b.shape) for b in back],
            out_specs=[constant(shape)] * 2,
        ),
        out_shape=[jax.ShapeDtypeStruct(shape, BF)] * 2,
        compiler_params=pltpu.CompilerParams(vmem_limit_bytes=32 * 1024 * 1024),
        cost_estimate=pl.CostEstimate(flops=1_000_000, bytes_accessed=4 << 20, transcendentals=0),
    )(info, *back)


def weight_kernel(lines, count, more, place, flags, *refs):
    xs, refs = refs[: lines * count], refs[lines * count :]
    grads, refs = refs[: lines * count], refs[lines * count :]
    before, refs = (refs[:lines], refs[lines:]) if more else (None, refs)
    outs, masked = refs[:lines], refs[lines]
    tiles = ROWS // ALIGN

    @pl.when(pl.program_id(0) == 0)
    def _():
        zero = jnp.zeros((ALIGN, HEAD), BF)
        for n in range(lines * count):
            for t in range(tiles):
                flag = flags[n * tiles + t]
                rows = grads[n][t * ALIGN : (t + 1) * ALIGN]
                span = slice(n * ROWS + t * ALIGN, n * ROWS + (t + 1) * ALIGN)
                masked[span, :HEAD] = jnp.where(flag == 1, rows, zero)
                masked[span, HEAD:] = jnp.where(flag == 1, zero, rows)

    for line in range(lines):
        total = None
        for n in range(line * count, (line + 1) * count):
            left = jnp.concatenate([xs[n][s, 0] for s in range(tiles)], axis=1)
            term = jnp.dot(left, masked[n * ROWS : (n + 1) * ROWS], preferred_element_type=F32)
            total = term if total is None else total + term
        if more:
            total = total + before[line][0].astype(F32)
        outs[line][0] = total.astype(BF)


def weight_part(info, lines, shifts, flags, turned, grads, before):
    count = len(shifts)
    sections, _, features, tile = turned[0].shape
    piece = features // SIDE
    width = 2 * HEAD

    def block(line, shift):
        return pl.BlockSpec(
            (sections, 1, piece, tile),
            lambda i, info, flags: (0, wrapped(info[3] * shift), wrapped(info[line] + info[3] * i), 0),
        )

    block_out = pl.BlockSpec((1, piece, width), lambda i, info, flags: (i, 0, 0))
    body = lambda *refs: weight_kernel(len(lines), count, bool(before), *refs)
    return pl.pallas_call(
        body,
        grid_spec=pltpu.PrefetchScalarGridSpec(
            num_scalar_prefetch=2,
            grid=(SIDE,),
            in_specs=[
                *[block(line, shift) for line in lines for shift in shifts],
                *[constant(g.shape) for g in grads],
                *[block_out] * len(before),
            ],
            out_specs=[block_out] * len(lines),
            scratch_shapes=[pltpu.VMEM((len(lines) * count * ROWS, width), BF)],
        ),
        out_shape=[jax.ShapeDtypeStruct((SIDE, piece, width), BF)] * len(lines),
        compiler_params=pltpu.CompilerParams(vmem_limit_bytes=56 * 1024 * 1024),
        cost_estimate=pl.CostEstimate(
            flops=2 * len(lines) * count * ROWS * features * width,
            bytes_accessed=len(lines) * (count * (2 << 20) + (3 << 20)),
            transcendentals=0,
        ),
    )(info, flags, *[turned[line] for line in lines for _ in shifts], *grads, *before)


def ring_near(value, moves):
    forth, back = moves
    return back(value), forth(value)


def ring_far(nearest, moves):
    following, previous = nearest
    forth, back = moves
    cut = following.shape[0] // 2
    return forth(previous[:cut]), back(following[cut:])


def ring_order(value, nearest, far, place):
    following, previous = nearest
    stack = [value[None], following[None], jnp.concatenate(far, axis=0)[None], previous[None]]
    return lax.dynamic_slice_in_dim(jnp.concatenate(stack * 2, axis=0), wrapped(-place), SIDE, 0)


def passing(ring_index, across):
    def move(value):
        pairs = []
        sections = lax.axis_size("sect")
        for member in range(SIDE * SIDE):
            for section in range(sections):
                place = [member // SIDE, member % SIDE]
                place[ring_index] = (place[ring_index] + (1 if section % 2 == 0 else -1)) % SIDE
                target = section ^ (sections // 2) if across else section
                pairs.append((member * sections + section, (place[0] * SIDE + place[1]) * sections + target))
        return lax.ppermute(value, ("seq", "sect"), pairs)

    return move


def pass_sums(lines, moves, moves_across):
    theirs = from_partner(jnp.concatenate([line[0][:, HEAD:] for line in lines], axis=1))
    going = [line[SIDE - 1] for line in lines]
    for n in range(SIDE - 2, 0, -1):
        came = [move(value) for move, value in zip(moves, going)]
        going = [(line[n].astype(F32) + value.astype(F32)).astype(BF) for line, value in zip(lines, came)]
    across = [move(value[:, HEAD:]) for move, value in zip(moves_across, going)]
    came = [move(value[:, :HEAD]) for move, value in zip(moves, going)]
    own = [line[0][:, :HEAD].astype(F32) + value.astype(F32) for line, value in zip(lines, came)]
    theirs = theirs.astype(F32) + jnp.concatenate(across, axis=1).astype(F32)
    return jnp.concatenate(own, axis=1), theirs


def unpacked(tile):
    return jnp.concatenate([tile[:, :HS], tile[:, HS:]], axis=0)


def after(values, *others):
    count = len(values)
    return list(lax.optimization_barrier((*values, *others))[:count])


def spread(pieces, ring):
    return [pieces[0]] + [lax.ppermute(pieces[d], "seq", ring(d)) for d in range(1, SIDE)]


def shards(tokens, image_spans, proj_weight, out_grad):
    section_count = lax.axis_size("sect")
    row_index = lax.axis_index("seq")
    place_y, place_z = row_index // SIDE, row_index % SIDE
    modality = lax.axis_index("sect") // (section_count // 2)
    up = 1 - 2 * (lax.axis_index("sect") % 2)
    info = jnp.stack([place_y, place_z, modality, up]).astype(jnp.int32)
    along_y, along_z = along(ring_y), along(ring_z)
    own_flags = (tile_flags(image_spans) == modality).astype(jnp.int32)

    weight = proj_weight[0]
    half_width = weight.shape[1] // 2
    slice_rows = weight.shape[0] // lax.axis_size("seq")
    sent = lax.dynamic_slice(
        weight, (row_index * slice_rows, (1 - modality) * half_width), (slice_rows, half_width)
    )
    got_weight = from_partner(sent)
    own_weight = lax.dynamic_slice_in_dim(weight, modality * half_width, half_width, 1)

    as_float = tokens.astype(F32)
    normed = (
        as_float * lax.rsqrt(jnp.mean(as_float * as_float, axis=1, keepdims=True) + EPSILON)
    ).astype(BF)
    gathered = lax.all_gather(normed, "sect", axis=0, tiled=True)

    turned = normed.T
    features, local_rows = turned.shape
    quarter = features // SIDE
    cube = turned.reshape(SIDE, SIDE, slice_rows, local_rows)

    def quarter_of(axis, place):
        return lax.dynamic_index_in_dim(cube, wrapped(place), axis, keepdims=False).reshape(quarter, local_rows)

    pieces_z = [quarter_of(1, place_z + d) for d in range(SIDE)]
    pieces_y = [quarter_of(0, place_y + d) for d in range(SIDE)]
    grads = []
    for d in range(SIDE):
        target = wrapped(place_z + d)
        first = (target + place_z) % 2 * CHUNK
        halves = [
            lax.dynamic_slice(out_grad, (first + n * (CHUNK // 2), target // 2 * HS), (CHUNK // 2, HS))
            for n in range(2)
        ]
        grads.append(jnp.concatenate(halves, axis=1))
    came_grad = spread(grads, ring_z)

    (got_weight,) = after([got_weight], *pieces_y, *pieces_z)
    one, two = got_weight[:, :HEAD], got_weight[:, HEAD:]
    near_a, near_b = ring_near(one, along_z), ring_near(two, along_y)
    far_a, far_b = ring_far(near_a, along_z), ring_far(near_b, along_y)
    line_a = ring_order(one, near_a, far_a, place_z)
    line_b = ring_order(two, near_b, far_b, place_y)
    near_a, near_b = ring_near(line_a, along_y), ring_near(line_b, along_z)
    near_a = after(near_a, own_weight)
    far_a, far_b = ring_far(near_a, along_y), ring_far(near_b, along_z)
    far_a = after(far_a, *came_grad)

    flags = lax.dynamic_index_in_dim(own_flags, row_index, 0, keepdims=False)
    came_z = spread(after(pieces_z, *far_a, *far_b), ring_z)
    sends = project(
        info, flags, gathered, own_weight, (line_a, *near_a), far_a, (line_b, *near_b), far_b
    )
    came_z = after(came_z, sends[0])
    turned_z = lax.all_gather(jnp.stack(came_z), "sect", axis=0)
    got = spread(sends, ring_z)
    came_y = spread(after(pieces_y, *got), ring_y)

    results = attention_pass(info, got, came_grad)
    came_y = after(came_y, results[0])
    turned_y = lax.all_gather(jnp.stack(came_y), "sect", axis=0)
    returned = spread(results[:SIDE], lambda d: ring_z(-d))
    grad_a, grad_b = assemble(info, returned)
    flag_cube = own_flags.reshape(SIDE, SIDE, -1)

    def add(lines, shifts, grads, before):
        flags = []
        for line in lines:
            for s in shifts:
                back = up * s
                flags.append(
                    flag_cube[place_y, wrapped(place_z - back)] if line == 0 else flag_cube[wrapped(place_y - back), place_z]
                )
        grads = [g[line] for line in lines for g in grads]
        return weight_part(info, lines, shifts, jnp.concatenate(flags), (turned_z, turned_y), grads, before)

    move_y, move_z = passing(0, False), passing(1, False)
    here = (grad_a, grad_b)
    next_1 = (move_z(here[0]), move_y(here[1]))
    next_2 = (move_z(next_1[0]), move_y(next_1[1]))
    part_z = add([0], [0, 1], [here, next_1], [])
    next_2 = after(next_2, *part_z)
    next_3 = (move_z(next_2[0]), move_y(next_2[1]))
    part_y = add([1], [0, 1], [here, next_1], [])
    next_3 = after(next_3, *part_y)
    parts = add([0, 1], [2, 3], [next_2, next_3], [*part_z, *part_y])
    own, theirs = pass_sums(parts, (move_y, move_z), (passing(0, True), passing(1, True)))
    lower = jnp.where(modality == 0, own, theirs)
    upper = jnp.where(modality == 0, theirs, own)
    grad_weight = jnp.concatenate([lower, upper], axis=1)[None]

    attended = spread(after(results[SIDE:], *next_2), lambda d: ring_z(-d))
    by_member = lax.dynamic_slice_in_dim(jnp.stack(attended * 2), wrapped(-place_z), SIDE, 0)
    swapped = place_z % 2

    def ordered(j):
        first, second = unpacked(by_member[2 * j]), unpacked(by_member[2 * j + 1])
        return jnp.where(
            swapped == 0,
            jnp.concatenate([first, second], axis=0),
            jnp.concatenate([second, first], axis=0),
        )

    attention = jnp.concatenate([ordered(j) for j in range(2)], axis=1)
    return (attention, grad_weight)


def solution(mesh):
    in_specs = (P(("seq", "sect"), None), P(), P("sect", None, None), P("seq", "sect"))
    out_specs = (P("seq", "sect"), P("sect", "seq", None))
    return jax.shard_map(shards, mesh=mesh, in_specs=in_specs, out_specs=out_specs, check_vma=False)
```

```python
import jax
import jax.numpy as jnp
from jax import lax
from jax.experimental import pallas as pl
from jax.experimental.pallas import tpu as pltpu
from jax.sharding import PartitionSpec as P

HS = 128
LEN = 4096
TILE_TOK = 256
ALIGN = 128
EPSILON = 1e-05
MASKED = -1e30
SIDE = 4
ROWS = LEN // SIDE
CHUNK = 512
HEAD = 3 * HS
LOG2E = 1.4426950408889634
BF = jnp.bfloat16
F32 = jnp.float32


def ring_z(step):
    return [(y * SIDE + z, y * SIDE + (z + step) % SIDE) for y in range(SIDE) for z in range(SIDE)]


def ring_y(step):
    return [(y * SIDE + z, (y + step) % SIDE * SIDE + z) for y in range(SIDE) for z in range(SIDE)]


def along(ring):
    return (
        lambda value: lax.ppermute(value, "seq", ring(1)),
        lambda value: lax.ppermute(value, "seq", ring(-1)),
    )


def from_partner(value):
    count = lax.axis_size("sect")
    return lax.ppermute(value, "sect", [(s, s ^ (count // 2)) for s in range(count)])


def tile_flags(image_spans):
    position = ALIGN * jnp.arange(LEN // ALIGN, dtype=jnp.int32)
    begins = image_spans[:, :, 0]
    beyond = begins + image_spans[:, :, 1] * TILE_TOK
    inside = (position[None, :, None] >= begins[:, None]) & (position[None, :, None] < beyond[:, None])
    return jnp.any(inside, axis=2).astype(jnp.int32).reshape(-1, ROWS // ALIGN)


def wrapped(value):
    return lax.rem(value + 2 * SIDE, SIDE)


def constant(shape):
    return pl.BlockSpec(shape, lambda i, *refs: (0,) * len(shape))


def project_kernel(info, flags, x, w, *refs):
    a_near, a_far, b_near, b_far = refs[0:3], refs[3:5], refs[5:8], refs[8:10]
    outs, total, other = refs[10:14], refs[14], refs[15]
    k = pl.program_id(0)
    place_y, place_z = info[0], info[1]
    quarter = ROWS
    small = quarter // SIDE
    shift = wrapped(k - place_y)
    for r, ref in ((0, a_near[0]), (1, a_near[1]), (3, a_near[2])):

        @pl.when(shift == r)
        def _(ref=ref):
            other[:, :HEAD] = ref[...].reshape(quarter, HEAD)

    @pl.when(shift == 2)
    def _():
        other[: quarter // 2, :HEAD] = a_far[0][...].reshape(quarter // 2, HEAD)
        other[quarter // 2 :, :HEAD] = a_far[1][...].reshape(quarter // 2, HEAD)

    for r, ref in ((0, b_near[0]), (1, b_near[1]), (3, b_near[2])):
        place = pl.multiple_of(wrapped(place_z + r) * small, small)
        other[pl.ds(place, small), HEAD:] = ref[k]
    place = pl.multiple_of(wrapped(place_z + 2) * small, small)

    @pl.when(k < SIDE // 2)
    def _():
        other[pl.ds(place, small), HEAD:] = b_far[0][lax.rem(k, 2)]

    @pl.when(k >= SIDE // 2)
    def _():
        other[pl.ds(place, small), HEAD:] = b_far[1][lax.rem(k, 2)]

    @pl.when(k == 0)
    def _():
        total[...] = jnp.zeros_like(total)

    own = w.at[pl.ds(pl.multiple_of(k * quarter, quarter), quarter)]

    @pl.loop(0, ROWS // (2 * ALIGN))
    def _(pair):
        one, two = flags[2 * pair], flags[2 * pair + 1]
        first = pl.multiple_of(pair * 2 * ALIGN, 2 * ALIGN)

        def add(start, count, weights):
            span = pl.ds(start, count)
            total[span] += jnp.dot(x[span], weights[...], preferred_element_type=F32)

        @pl.when((one == 1) & (two == 1))
        def _():
            add(first, 2 * ALIGN, own)

        @pl.when((one == 0) & (two == 0))
        def _():
            add(first, 2 * ALIGN, other)

        @pl.when((one == 1) & (two == 0))
        def _():
            add(first, ALIGN, own)
            add(first + ALIGN, ALIGN, other)

        @pl.when((one == 0) & (two == 1))
        def _():
            add(first, ALIGN, other)
            add(first + ALIGN, ALIGN, own)

    @pl.when(k == SIDE - 1)
    def _():
        for d in range(SIDE):
            target = wrapped(place_z + d)
            part = lax.rem(target + place_z, 2)
            for h in range(2):

                @pl.when(target // 2 == h)
                def _(d=d, h=h, part=part):
                    outs[d][:ROWS] = total[:, h * HEAD + HS : (h + 1) * HEAD].astype(BF)
                    for side in range(2):
                        start = pl.multiple_of(part * CHUNK + side * (CHUNK // 2), CHUNK // 2)
                        outs[d][ROWS:, side * HS : (side + 1) * HS] = total[
                            pl.ds(start, CHUNK // 2), h * HEAD : h * HEAD + HS
                        ].astype(BF)


def project(info, flags, gathered, own_weight, near_a, far_a, near_b, far_b):
    rows, features = gathered.shape
    width = 2 * HEAD
    step = features // SIDE
    packed = (ROWS + CHUNK // 2, 2 * HS)
    pieces = [*near_a, *far_a, *near_b, *far_b]
    return pl.pallas_call(
        project_kernel,
        grid_spec=pltpu.PrefetchScalarGridSpec(
            num_scalar_prefetch=2,
            grid=(SIDE,),
            in_specs=[
                pl.BlockSpec((rows, step), lambda k, info, flags: (0, k)),
                constant(own_weight.shape),
                *[constant(p.shape) for p in pieces],
            ],
            out_specs=[constant(packed)] * SIDE,
            scratch_shapes=[pltpu.VMEM((rows, width), F32), pltpu.VMEM((step, width), BF)],
        ),
        out_shape=[jax.ShapeDtypeStruct(packed, BF)] * SIDE,
        compiler_params=pltpu.CompilerParams(vmem_limit_bytes=58 * 1024 * 1024),
        cost_estimate=pl.CostEstimate(
            flops=2 * rows * features * width, bytes_accessed=22 << 20, transcendentals=0
        ),
    )(info, flags, gathered, own_weight, *pieces)


def attention_kernel(info, *refs):
    got, grad_refs, backs, out_refs = (refs[n * SIDE : (n + 1) * SIDE] for n in range(4))
    key_rows, value_rows, q_rows, g_rows, score, out_t, dq_t, dk_sum, dv_sum = refs[4 * SIDE :]
    step = pl.program_id(0)
    place = info[1]
    half = lax.rem(place, 2)
    source = wrapped(place - step)
    chunk = 2 * source + lax.rem(source + half, 2)
    factor = HS ** (-0.5)

    @pl.when(step == 0)
    def _():
        dk_sum[...] = jnp.zeros_like(dk_sum)
        dv_sum[...] = jnp.zeros_like(dv_sum)
        for d in range(SIDE):
            span = pl.ds(pl.multiple_of(wrapped(place - d) * ROWS, ROWS), ROWS)
            key_rows[span] = got[d][:ROWS, :HS]
            value_rows[span] = got[d][:ROWS, HS:]

    for d in range(SIDE):

        @pl.when(step == d)
        def _(d=d):
            q_rows[: CHUNK // 2] = got[d][ROWS:, :HS]
            q_rows[CHUNK // 2 :] = got[d][ROWS:, HS:]
            g_rows[: CHUNK // 2] = grad_refs[d][:, :HS]
            g_rows[CHUNK // 2 :] = grad_refs[d][:, HS:]

    q = q_rows[...]
    grad = g_rows[...]

    def span_of(j):
        return pl.ds(pl.multiple_of(j * CHUNK, CHUNK), CHUNK)

    def raw(j):
        return lax.dot_general(
            key_rows[span_of(j)], q, (((1,), (1,)), ((), ())), preferred_element_type=F32
        )

    def first_pass(j, top):
        s = raw(j)
        score[j] = s
        return jnp.maximum(top, jnp.max(s, axis=0, keepdims=True))

    diagonal = raw(chunk)
    allowed = lax.broadcasted_iota(jnp.int32, (CHUNK, CHUNK), 0) <= lax.broadcasted_iota(
        jnp.int32, (CHUNK, CHUNK), 1
    )
    diagonal = jnp.where(allowed, diagonal, MASKED)
    score[chunk] = diagonal
    top = lax.fori_loop(0, chunk, first_pass, jnp.max(diagonal, axis=0, keepdims=True))
    out_t[...] = jnp.zeros_like(out_t)

    def second_pass(j, total):
        p = jnp.exp2((score[j] - top) * (factor * LOG2E))
        score[j] = p
        out_t[...] += lax.dot_general(
            value_rows[span_of(j)], p.astype(BF), (((0,), (0,)), ((), ())), preferred_element_type=F32
        )
        return total + jnp.sum(p, axis=0, keepdims=True)

    total = lax.fori_loop(0, chunk + 1, second_pass, jnp.zeros((1, CHUNK), F32))
    inverse = 1.0 / total
    attended = (out_t[...] * inverse).astype(BF).astype(F32)
    grad_t = grad.astype(F32).T
    row_dot = jnp.sum(attended * grad_t, axis=0, keepdims=True)
    attended = attended.T.astype(BF)
    dq_t[...] = jnp.zeros_like(dq_t)

    def third_pass(j, carry):
        p = score[j] * inverse
        span = span_of(j)
        dv_sum[span] += jnp.dot(p.astype(BF), grad, preferred_element_type=F32)
        dp = lax.dot_general(
            value_rows[span], grad, (((1,), (1,)), ((), ())), preferred_element_type=F32
        )
        ds = (p * (dp - row_dot)).astype(BF)
        dk_sum[span] += jnp.dot(ds, q, preferred_element_type=F32)
        dq_t[...] += lax.dot_general(
            key_rows[span], ds, (((0,), (0,)), ((), ())), preferred_element_type=F32
        )
        return carry

    lax.fori_loop(0, chunk + 1, third_pass, 0)
    dq = (dq_t[...] * factor).T.astype(BF)
    for d in range(SIDE):

        @pl.when(step == d)
        def _(d=d):
            backs[d][ROWS:, :HS] = dq[: CHUNK // 2]
            backs[d][ROWS:, HS:] = dq[CHUNK // 2 :]
            out_refs[d][:, :HS] = attended[: CHUNK // 2]
            out_refs[d][:, HS:] = attended[CHUNK // 2 :]

    @pl.when(step == SIDE - 1)
    def _():
        for d in range(SIDE):
            span = pl.ds(pl.multiple_of(wrapped(place - d) * ROWS, ROWS), ROWS)
            backs[d][:ROWS, :HS] = (dk_sum[span] * factor).astype(BF)
            backs[d][:ROWS, HS:] = dv_sum[span].astype(BF)


def attention_pass(info, got, grad):
    shape, small = got[0].shape, (CHUNK // 2, 2 * HS)
    return pl.pallas_call(
        attention_kernel,
        grid_spec=pltpu.PrefetchScalarGridSpec(
            num_scalar_prefetch=1,
            grid=(SIDE,),
            in_specs=[constant(shape)] * SIDE + [constant(small)] * SIDE,
            out_specs=[constant(shape)] * SIDE + [constant(small)] * SIDE,
            scratch_shapes=[
                pltpu.VMEM((LEN, HS), BF),
                pltpu.VMEM((LEN, HS), BF),
                pltpu.VMEM((CHUNK, HS), BF),
                pltpu.VMEM((CHUNK, HS), BF),
                pltpu.VMEM((LEN // CHUNK, CHUNK, CHUNK), F32),
                pltpu.VMEM((HS, CHUNK), F32),
                pltpu.VMEM((HS, CHUNK), F32),
                pltpu.VMEM((LEN, HS), F32),
                pltpu.VMEM((LEN, HS), F32),
            ],
        ),
        out_shape=[jax.ShapeDtypeStruct(shape, BF)] * SIDE + [jax.ShapeDtypeStruct(small, BF)] * SIDE,
        compiler_params=pltpu.CompilerParams(vmem_limit_bytes=58 * 1024 * 1024),
        cost_estimate=pl.CostEstimate(
            flops=28_000_000_000, bytes_accessed=7_000_000, transcendentals=5_000_000
        ),
    )(info, *got, *grad)


def assemble_kernel(info, *refs):
    back, outs = refs[:SIDE], refs[SIDE:]
    for z in range(SIDE):

        @pl.when(info[1] == z)
        def _(z=z):
            ordered = [back[(i - z) % SIDE] for i in range(SIDE)]
            for h in range(2):
                pair = ordered[2 * h : 2 * h + 2]
                outs[h][:, HS:] = (pair[0][:ROWS].astype(F32) + pair[1][:ROWS].astype(F32)).astype(BF)
                for part in range(2):
                    tile = pair[(part + z) % 2]
                    for side in range(2):
                        start = part * CHUNK + side * (CHUNK // 2)
                        outs[h][start : start + CHUNK // 2, :HS] = tile[ROWS:, side * HS : (side + 1) * HS]


def assemble(info, back):
    shape = (ROWS, HEAD)
    return pl.pallas_call(
        assemble_kernel,
        grid_spec=pltpu.PrefetchScalarGridSpec(
            num_scalar_prefetch=1,
            grid=(1,),
            in_specs=[constant(b.shape) for b in back],
            out_specs=[constant(shape)] * 2,
        ),
        out_shape=[jax.ShapeDtypeStruct(shape, BF)] * 2,
        compiler_params=pltpu.CompilerParams(vmem_limit_bytes=32 * 1024 * 1024),
        cost_estimate=pl.CostEstimate(flops=1_000_000, bytes_accessed=4 << 20, transcendentals=0),
    )(info, *back)


def weight_kernel(lines, count, more, place, flags, *refs):
    xs, refs = refs[: lines * count], refs[lines * count :]
    grads, refs = refs[: lines * count], refs[lines * count :]
    before, refs = (refs[:lines], refs[lines:]) if more else (None, refs)
    outs, masked = refs[:lines], refs[lines]
    tiles = ROWS // ALIGN

    @pl.when(pl.program_id(0) == 0)
    def _():
        zero = jnp.zeros((ALIGN, HEAD), BF)
        for n in range(lines * count):
            for t in range(tiles):
                flag = flags[n * tiles + t]
                rows = grads[n][t * ALIGN : (t + 1) * ALIGN]
                span = slice(n * ROWS + t * ALIGN, n * ROWS + (t + 1) * ALIGN)
                masked[span, :HEAD] = jnp.where(flag == 1, rows, zero)
                masked[span, HEAD:] = jnp.where(flag == 1, zero, rows)

    for line in range(lines):
        total = None
        for n in range(line * count, (line + 1) * count):
            left = jnp.concatenate([xs[n][s, 0] for s in range(tiles)], axis=1)
            term = jnp.dot(left, masked[n * ROWS : (n + 1) * ROWS], preferred_element_type=F32)
            total = term if total is None else total + term
        if more:
            total = total + before[line][0].astype(F32)
        outs[line][0] = total.astype(BF)


def weight_part(info, lines, shifts, flags, turned, grads, before):
    count = len(shifts)
    sections, _, features, tile = turned[0].shape
    piece = features // SIDE
    width = 2 * HEAD

    def block(line, shift):
        return pl.BlockSpec(
            (sections, 1, piece, tile),
            lambda i, info, flags: (0, wrapped(info[3] * shift), wrapped(info[line] + info[3] * i), 0),
        )

    block_out = pl.BlockSpec((1, piece, width), lambda i, info, flags: (i, 0, 0))
    body = lambda *refs: weight_kernel(len(lines), count, bool(before), *refs)
    return pl.pallas_call(
        body,
        grid_spec=pltpu.PrefetchScalarGridSpec(
            num_scalar_prefetch=2,
            grid=(SIDE,),
            in_specs=[
                *[block(line, shift) for line in lines for shift in shifts],
                *[constant(g.shape) for g in grads],
                *[block_out] * len(before),
            ],
            out_specs=[block_out] * len(lines),
            scratch_shapes=[pltpu.VMEM((len(lines) * count * ROWS, width), BF)],
        ),
        out_shape=[jax.ShapeDtypeStruct((SIDE, piece, width), BF)] * len(lines),
        compiler_params=pltpu.CompilerParams(vmem_limit_bytes=56 * 1024 * 1024),
        cost_estimate=pl.CostEstimate(
            flops=2 * len(lines) * count * ROWS * features * width,
            bytes_accessed=len(lines) * (count * (2 << 20) + (3 << 20)),
            transcendentals=0,
        ),
    )(info, flags, *[turned[line] for line in lines for _ in shifts], *grads, *before)


def ring_near(value, moves):
    forth, back = moves
    return back(value), forth(value)


def ring_far(nearest, moves):
    following, previous = nearest
    forth, back = moves
    cut = following.shape[0] // 2
    return forth(previous[:cut]), back(following[cut:])


def ring_order(value, nearest, far, place):
    following, previous = nearest
    stack = [value[None], following[None], jnp.concatenate(far, axis=0)[None], previous[None]]
    return lax.dynamic_slice_in_dim(jnp.concatenate(stack * 2, axis=0), wrapped(-place), SIDE, 0)


def passing(ring_index, across):
    def move(value):
        pairs = []
        sections = lax.axis_size("sect")
        for member in range(SIDE * SIDE):
            for section in range(sections):
                place = [member // SIDE, member % SIDE]
                place[ring_index] = (place[ring_index] + (1 if section % 2 == 0 else -1)) % SIDE
                target = section ^ (sections // 2) if across else section
                pairs.append((member * sections + section, (place[0] * SIDE + place[1]) * sections + target))
        return lax.ppermute(value, ("seq", "sect"), pairs)

    return move


def pass_sums(lines, moves, moves_across):
    theirs = from_partner(jnp.concatenate([line[0][:, HEAD:] for line in lines], axis=1))
    going = [line[SIDE - 1] for line in lines]
    for n in range(SIDE - 2, 0, -1):
        came = [move(value) for move, value in zip(moves, going)]
        going = [(line[n].astype(F32) + value.astype(F32)).astype(BF) for line, value in zip(lines, came)]
    across = [move(value[:, HEAD:]) for move, value in zip(moves_across, going)]
    came = [move(value[:, :HEAD]) for move, value in zip(moves, going)]
    own = [line[0][:, :HEAD].astype(F32) + value.astype(F32) for line, value in zip(lines, came)]
    theirs = theirs.astype(F32) + jnp.concatenate(across, axis=1).astype(F32)
    return jnp.concatenate(own, axis=1), theirs


def unpacked(tile):
    return jnp.concatenate([tile[:, :HS], tile[:, HS:]], axis=0)


def after(values, *others):
    count = len(values)
    return list(lax.optimization_barrier((*values, *others))[:count])


def spread(pieces, ring):
    return [pieces[0]] + [lax.ppermute(pieces[d], "seq", ring(d)) for d in range(1, SIDE)]


def shards(tokens, image_spans, proj_weight, out_grad):
    section_count = lax.axis_size("sect")
    row_index = lax.axis_index("seq")
    place_y, place_z = row_index // SIDE, row_index % SIDE
    modality = lax.axis_index("sect") // (section_count // 2)
    up = 1 - 2 * (lax.axis_index("sect") % 2)
    info = jnp.stack([place_y, place_z, modality, up]).astype(jnp.int32)
    along_y, along_z = along(ring_y), along(ring_z)
    own_flags = (tile_flags(image_spans) == modality).astype(jnp.int32)

    weight = proj_weight[0]
    half_width = weight.shape[1] // 2
    slice_rows = weight.shape[0] // lax.axis_size("seq")
    sent = lax.dynamic_slice(
        weight, (row_index * slice_rows, (1 - modality) * half_width), (slice_rows, half_width)
    )
    got_weight = from_partner(sent)
    own_weight = lax.dynamic_slice_in_dim(weight, modality * half_width, half_width, 1)

    as_float = tokens.astype(F32)
    normed = (
        as_float * lax.rsqrt(jnp.mean(as_float * as_float, axis=1, keepdims=True) + EPSILON)
    ).astype(BF)
    gathered = lax.all_gather(normed, "sect", axis=0, tiled=True)

    turned = normed.T
    features, local_rows = turned.shape
    quarter = features // SIDE
    cube = turned.reshape(SIDE, SIDE, slice_rows, local_rows)

    def quarter_of(axis, place):
        return lax.dynamic_index_in_dim(cube, wrapped(place), axis, keepdims=False).reshape(quarter, local_rows)

    pieces_z = [quarter_of(1, place_z + d) for d in range(SIDE)]
    pieces_y = [quarter_of(0, place_y + d) for d in range(SIDE)]
    grads = []
    for d in range(SIDE):
        target = wrapped(place_z + d)
        first = (target + place_z) % 2 * CHUNK
        halves = [
            lax.dynamic_slice(out_grad, (first + n * (CHUNK // 2), target // 2 * HS), (CHUNK // 2, HS))
            for n in range(2)
        ]
        grads.append(jnp.concatenate(halves, axis=1))
    came_grad = spread(grads, ring_z)

    (got_weight,) = after([got_weight], *pieces_z)
    one, two = got_weight[:, :HEAD], got_weight[:, HEAD:]
    near_a, near_b = ring_near(one, along_z), ring_near(two, along_y)
    far_a, far_b = ring_far(near_a, along_z), ring_far(near_b, along_y)
    line_a = ring_order(one, near_a, far_a, place_z)
    line_b = ring_order(two, near_b, far_b, place_y)
    near_a, near_b = ring_near(line_a, along_y), ring_near(line_b, along_z)
    near_a = after(near_a, own_weight, *pieces_y)
    far_a, far_b = ring_far(near_a, along_y), ring_far(near_b, along_z)
    far_a = after(far_a, *came_grad)

    flags = lax.dynamic_index_in_dim(own_flags, row_index, 0, keepdims=False)
    came_z = spread(after(pieces_z, *far_a, *far_b), ring_z)
    sends = project(
        info, flags, gathered, own_weight, (line_a, *near_a), far_a, (line_b, *near_b), far_b
    )
    came_z = after(came_z, sends[0])
    turned_z = lax.all_gather(jnp.stack(came_z), "sect", axis=0)
    got = spread(sends, ring_z)
    came_y = spread(after(pieces_y, *got), ring_y)

    results = attention_pass(info, got, came_grad)
    came_y = after(came_y, results[0])
    turned_y = lax.all_gather(jnp.stack(came_y), "sect", axis=0)
    returned = spread(results[:SIDE], lambda d: ring_z(-d))
    grad_a, grad_b = assemble(info, returned)
    flag_cube = own_flags.reshape(SIDE, SIDE, -1)

    def add(lines, shifts, grads, before):
        flags = []
        for line in lines:
            for s in shifts:
                back = up * s
                flags.append(
                    flag_cube[place_y, wrapped(place_z - back)] if line == 0 else flag_cube[wrapped(place_y - back), place_z]
                )
        grads = [g[line] for line in lines for g in grads]
        return weight_part(info, lines, shifts, jnp.concatenate(flags), (turned_z, turned_y), grads, before)

    move_y, move_z = passing(0, False), passing(1, False)
    here = (grad_a, grad_b)
    next_1 = (move_z(here[0]), move_y(here[1]))
    next_2 = (move_z(next_1[0]), move_y(next_1[1]))
    part_z = add([0], [0, 1], [here, next_1], [])
    next_2 = after(next_2, *part_z)
    next_3 = (move_z(next_2[0]), move_y(next_2[1]))
    part_y = add([1], [0, 1], [here, next_1], [])
    next_3 = after(next_3, *part_y)
    parts = add([0, 1], [2, 3], [next_2, next_3], [*part_z, *part_y])
    own, theirs = pass_sums(parts, (move_y, move_z), (passing(0, True), passing(1, True)))
    lower = jnp.where(modality == 0, own, theirs)
    upper = jnp.where(modality == 0, theirs, own)
    grad_weight = jnp.concatenate([lower, upper], axis=1)[None]

    attended = spread(after(results[SIDE:], *next_2), lambda d: ring_z(-d))
    by_member = lax.dynamic_slice_in_dim(jnp.stack(attended * 2), wrapped(-place_z), SIDE, 0)
    swapped = place_z % 2

    def ordered(j):
        first, second = unpacked(by_member[2 * j]), unpacked(by_member[2 * j + 1])
        return jnp.where(
            swapped == 0,
            jnp.concatenate([first, second], axis=0),
            jnp.concatenate([second, first], axis=0),
        )

    attention = jnp.concatenate([ordered(j) for j in range(2)], axis=1)
    return (attention, grad_weight)


def solution(mesh):
    in_specs = (P(("seq", "sect"), None), P(), P("sect", None, None), P("seq", "sect"))
    out_specs = (P("seq", "sect"), P("sect", "seq", None))
    return jax.shard_map(shards, mesh=mesh, in_specs=in_specs, out_specs=out_specs, check_vma=False)
```
